512 devices in a mesh: mem: 16 (over x, z_lo), lat: 4 (over z_hi), win: 8 (over y, core).
Axes of the slice: x: 4, y: 4, z: 16 (z_hi: 4, z_lo: 4; z = z_hi * 4 + z_lo), core: 2. Of those that a mesh axis runs over, the one named last changes fastest.
Arguments:
- ensemble: float32 [32, 8, 32, 2048], P('mem', None, 'lat'), may hold values from -6 to 6
- weights: float32 [8, 32, 32, 2048], P('win', 'mem', 'lat'), may hold values from -6 to 6
- diffusivity: float32 [8, 32, 2048], P(None, 'lat', 'mem'), may hold values from 0.05 to 0.4
- coupling: float32 [8, 8], replicated, may hold values from -0.5 to 0.5
- tl_steps: int32 [8], P('win'), may hold values from 1 to 6
- obs_cell: int32 [65536], P(('mem', 'lat')), may hold values from 0 to 8191
- obs_window: int32 [65536], P(('mem', 'lat')), may hold values from 0 to 7
- obs_value: float32 [65536], P(('mem', 'lat')), may hold values from -6 to 6
- obs_weight: float32 [65536], P(('mem', 'lat')), may hold values from 1 to 8
- error_weight: float32 [8], replicated, may hold values from 0.5 to 4
Outputs:
- control: float32 [8, 32, 32, 2048], P('win', 'mem', 'lat')
- increment: float32 [8, 8, 32, 2048], P('win', None, 'lat', 'mem')
The draws below stay inside these ranges and needn't reach their ends.
Inputs may be any that keep to these rules, and one draw needn't show every extreme that they name: `tl_steps`: how many of the 6 tangent steps the subwindow takes. `obs_cell`: index of the observed cell in the block of 8 x 8 x 128 cells that the observation's device holds (mem index, lat index), flattened as variable, row, longitude.
All inputs are finite; a program needn't handle non-finite values.
Results may differ from the reference program's by a relative error of at most 0.00015.
Values sent between devices are 32-bit elements; how exact they have to be, the bound alone decides.
A program may use at most 64 MiB of HBM per device.

```python
import math
import jax
import jax.numpy as jnp
from jax import lax

NV = 8
LB = 8
LON_DEV = 128
OBS_DEV = 1024
KMAX = 6
DIFF = 2
ITERS = 2
M = 32
NLAT = 32
NLON = 2048
NWIN = 8
NOBS = 65536
N_MEM = 16
N_LAT = 4
N_WIN = 8


def touch_ends(array, own_key, smallest, high):
    index_at = [jax.random.randint(jax.random.fold_in(own_key, axis), (), 0, length) for axis, length in enumerate(array.shape)]
    longest = array.shape.index(max(array.shape))
    beside = index_at[:longest] + [(index_at[longest] + 1) % array.shape[longest]] + index_at[longest + 1:]
    return array.at[tuple(index_at)].set(smallest).at[tuple(beside)].set(high)


def shard_levels(key, extent, shards, low, top_value):
    gain, own = 1.0, jax.random.fold_in(key, 6)
    for position, parts in shards:
        steps = jnp.exp(jax.random.uniform(jax.random.fold_in(own, position), (parts,), jnp.float32, low / len(shards), top_value / len(shards)))
        gain = gain * jnp.repeat(steps, extent[position] // parts).reshape([-1 if axis == position else 1 for axis in range(len(extent))])
    return gain


def scatter_about(key, dims, width, limit, split=(), held_as=jnp.bfloat16):
    array = jax.random.normal(key, dims, jnp.float32) * width
    if len(split) > 0:
        array = shard_levels(key, dims, split, -0.22, 0.18) * array
    return jnp.clip(array, min=-limit, max=limit).astype(held_as)


def setup_inputs(seed: int = 0) -> dict:
    keys = jax.random.split(jax.random.key(seed), 11)
    ensemble = scatter_about(keys[0], (M, NV, NLAT, NLON), 1.0, 6.0, ((0, 16), (2, 4)), jnp.float32)
    weights = scatter_about(keys[1], (NWIN, M, NLAT, NLON), 1.0, 6.0, ((0, 8), (1, 16), (2, 4)), jnp.float32)
    diffusivity = jnp.clip(jnp.exp(math.log(0.4) - 2.0794415 * jax.random.uniform(keys[2], (NV, NLAT, NLON), jnp.float32) ** shard_levels(keys[2], (NV, NLAT, NLON), ((1, 4), (2, 16)), -0.2, 0.2)), 0.05, 0.4)
    coupling = scatter_about(keys[3], (NV, NV), 0.1, 0.5, (), jnp.float32)
    tl_steps = touch_ends(jax.random.randint(keys[4], (NWIN,), 1, KMAX + 1), jax.random.fold_in(keys[4], 1), 1, KMAX).astype(jnp.int32)
    obs_cell = touch_ends(jax.random.randint(keys[5], (NOBS,), 0, NV * LB * LON_DEV), jax.random.fold_in(keys[5], 1), 0, (NV * LB * LON_DEV) - 1).astype(jnp.int32)
    obs_window = touch_ends(jax.random.randint(keys[6], (NOBS,), 0, NWIN), jax.random.fold_in(keys[6], 1), 0, NWIN - 1).astype(jnp.int32)
    obs_value = scatter_about(keys[7], (NOBS,), 1.0, 6.0, ((0, 64),), jnp.float32)
    obs_weight = jnp.clip(jnp.exp(math.log(8.0) - 2.0794415 * jax.random.uniform(keys[8], (NOBS,), jnp.float32) ** shard_levels(keys[8], (NOBS,), ((0, 64),), -0.2, 0.2)), 1.0, 8.0)
    error_weight = jnp.clip(jnp.exp(jax.random.uniform(keys[9], (NV,), jnp.float32, math.log(0.5), math.log(4.0))), 0.5, 4.0)
    return dict(ensemble=ensemble, weights=weights, diffusivity=diffusivity, coupling=coupling, tl_steps=tl_steps, obs_cell=obs_cell, obs_window=obs_window, obs_value=obs_value, obs_weight=obs_weight, error_weight=error_weight)


KAPPA = 0.125
DESCENT = 0.25
HIGHEST = lax.Precision.HIGHEST

def relax(padded):
    middle = padded[..., 1:-1, :]
    beside_all = padded[..., 2:, :] + padded[..., :-2, :] + jnp.roll(middle, 1, -1) + jnp.roll(middle, -1, -1)
    return middle + KAPPA * (beside_all - 4.0 * middle)

def diffuse(values):
    widths = [(0, 0)] * (values.ndim - 2) + [(1, 1), (0, 0)]
    for repeat in range(DIFF):
        values = relax(jnp.pad(values, widths))
    return values

def forward(state, diffusivity, coupling, tl_steps):
    for section_index in range(KMAX):
        padded = jnp.pad(state, ((0, 0), (0, 0), (1, 1), (0, 0)))
        second = padded[:, :, 2:] + padded[:, :, :-2] - 2.0 * state
        mixed = jnp.einsum('vu,wurl->wvrl', coupling, state, precision=HIGHEST)
        moved = state + diffusivity[None] * second + mixed
        state = jnp.where((section_index < tl_steps)[:, None, None, None], moved, state)
    return state

def backward(state, diffusivity, coupling, tl_steps):
    for section_index in reversed(range(KMAX)):
        weighted = diffusivity[None] * state
        padded = jnp.pad(weighted, ((0, 0), (0, 0), (1, 1), (0, 0)))
        second = padded[:, :, 2:] + padded[:, :, :-2] - 2.0 * weighted
        mixed = jnp.einsum('uv,wurl->wvrl', coupling, state, precision=HIGHEST)
        moved = state + second + mixed
        state = jnp.where((section_index < tl_steps)[:, None, None, None], moved, state)
    return state

def observe(ends, obs_cell, obs_window, obs_value, obs_weight):
    nblock = N_MEM * N_LAT
    blocks = ends.reshape(N_WIN, NV, N_LAT, LB, N_MEM, LON_DEV).transpose(0, 4, 2, 1, 3, 5).reshape(N_WIN, nblock, NV * LB * LON_DEV)
    cells = obs_cell.reshape(nblock, OBS_DEV)
    picked = jnp.take_along_axis(blocks, cells[None], axis=2)
    window_ids = jnp.arange(N_WIN, dtype=jnp.int32)
    chosen = obs_window.reshape(nblock, OBS_DEV)[None] == window_ids[:, None, None]
    innovation = jnp.where(chosen, (picked - obs_value.reshape(nblock, OBS_DEV)[None]) * obs_weight.reshape(nblock, OBS_DEV)[None], 0.0)
    block_rows = jnp.arange(nblock, dtype=jnp.int32)[:, None]
    spread = jnp.zeros_like(blocks).at[:, block_rows, cells].add(innovation)
    return spread.reshape(N_WIN, N_MEM, N_LAT, NV, LB, LON_DEV).transpose(0, 3, 2, 4, 1, 5).reshape(N_WIN, NV, NLAT, NLON)

def reference(ensemble, weights, diffusivity, coupling, tl_steps, obs_cell, obs_window, obs_value, obs_weight, error_weight):
    member_scale = 1.0 / math.sqrt(M - 1)
    control = weights
    has_before = (jnp.arange(N_WIN) > 0)[:, None, None, None]
    increment = None
    for iteration in range(ITERS):
        smoothed = diffuse(control)
        increment = jnp.einsum('mvrl,wmrl->wvrl', ensemble, smoothed, precision=HIGHEST) * member_scale
        ends = forward(increment, diffusivity, coupling, tl_steps)
        previous = jnp.concatenate([jnp.zeros_like(ends[:1]), ends[:-1]], 0)
        misfit = jnp.where(has_before, error_weight[None, :, None, None] * (previous - increment), 0.0)
        misfit_next = jnp.concatenate([misfit[1:], jnp.zeros_like(misfit[:1])], 0)
        observed = observe(ends, obs_cell, obs_window, obs_value, obs_weight)
        gradient = backward(observed + misfit_next, diffusivity, coupling, tl_steps) - misfit
        back_members = jnp.einsum('mvrl,wvrl->wmrl', ensemble, gradient, precision=HIGHEST) * member_scale
        control = control - DESCENT * (control + diffuse(back_members))
    return (control, increment)
```

```python
import functools
import math

import jax
import jax.numpy as jnp
from jax import lax
from jax.experimental import pallas as pl
from jax.experimental.pallas import tpu as pltpu
from jax.sharding import PartitionSpec as P

MESH = pl.DeviceIdType.MESH
NV = 8
LB = 8
LANES = 128
KMAX = 6
ITERS = 2
KAPPA = 0.125
DESCENT = 0.25
KEEP = 1.0 - DESCENT
CENTER = 1.0 - 4.0 * KAPPA
GROUP = 4
F32 = jnp.float32


def start_to(src, dst, send_sem, recv_sem, mem, lat, win):
    pltpu.make_async_remote_copy(
        src_ref=src,
        dst_ref=dst,
        send_sem=send_sem,
        recv_sem=recv_sem,
        device_id={"mem": mem, "lat": lat, "win": win},
        device_id_type=MESH,
    ).start()


def drain(ref, sem):
    pltpu.make_async_copy(ref, ref, sem).wait()


def along(f, lon):
    return CENTER * f + KAPPA * (pltpu.roll(f, 1, 1) + pltpu.roll(f, lon - 1, 1))


def kernel(
    nm,
    nl,
    nw,
    e_hbm,
    c_hbm,
    d_hbm,
    coup,
    steps,
    obs_cell,
    obs_window,
    obs_value,
    obs_weight,
    err_w,
    ctl_out,
    inc_out,
    et,
    cbuf,
    sm,
    s_top,
    s_bot,
    s_in,
    r_top,
    r_bot,
    dif,
    fstate,
    bstate,
    inc_next,
    ends_own,
    ends_prev,
    wv,
    ewb,
    b1,
    ts,
    bs,
    rt,
    rb,
    pk,
    pkt,
    pkb,
    rx,
    rxt,
    rxb,
    pfull,
    ext,
    sq,
    bsum,
    o_top,
    o_bot,
    c_in,
    c_top,
    c_bot,
    local,
    e_send,
    e_recv,
    y_send,
    y_recv,
    k_send,
    k_recv,
    s_send,
    s_recv,
    d_send,
    d_recv,
    f_send,
    f_recv,
    w_send,
    w_recv,
    h_send,
    h_recv,
    o_send,
    o_recv,
):
    m, b, w = lax.axis_index("mem"), lax.axis_index("lat"), lax.axis_index("win")
    members = 2 * nm
    lon = nm * LANES
    vp = NV // nw
    scale = 1.0 / math.sqrt(members - 1)
    up, down = b > 0, b < nl - 1
    before, after = w > 0, w < nw - 1
    other = w + 1 - 2 * lax.rem(w, 2)
    planes = nw // 2
    left, right = lax.rem(m + nm - 1, nm), lax.rem(m + 1, nm)
    mine = pl.ds(pl.multiple_of(m * LANES, LANES), LANES)
    my_pair = pl.ds(2 * m, 2)
    my_piece = pl.ds(w * vp, vp)

    load_c = pltpu.make_async_copy(c_hbm.at[0], cbuf, local.at[0])
    load_c.start()
    load_d = pltpu.make_async_copy(d_hbm, dif.at[1], local.at[1])
    load_d.start()
    for i in range(vp):
        pltpu.make_async_copy(
            e_hbm.at[:, w * vp + i, :, mine], et.at[w * vp + i, my_pair], local.at[2]
        ).start()

    barrier = pltpu.get_barrier_semaphore()

    def hello(mem, lat, win):
        pl.semaphore_signal(
            barrier, inc=1, device_id={"mem": mem, "lat": lat, "win": win}, device_id_type=MESH
        )

    def greet(k, _):
        to = lax.rem(m + k, nm)

        @pl.when(k > 0)
        def _():
            hello(to, b, w)

        @pl.when(up)
        def _():
            hello(to, b - 1, w)

        @pl.when(down)
        def _():
            hello(to, b + 1, w)

        return 0

    lax.fori_loop(0, nm, greet, 0)
    for k in range(1, planes):
        hello(m, b, lax.rem(w + 2 * k, nw))
    hello(m, b, other)
    odd = lax.rem(w, 2)

    @pl.when((odd == 0) & before)
    def _():
        hello(m, b, w - 1)

    @pl.when((odd == 1) & after)
    def _():
        hello(m, b, w + 1)

    one_more = jnp.where((w > 0) & (w < nw - 1), 1, 0)
    bands = jnp.where(up, 1, 0) + jnp.where(down, 1, 0)
    pl.semaphore_wait(barrier, nm - 1 + nm * bands + planes + one_more)

    def send_e(k, _):
        to = lax.rem(m + k, nm)
        for i in range(vp):
            start_to(
                e_hbm.at[:, w * vp + i, :, pl.ds(pl.multiple_of(to * LANES, LANES), LANES)],
                et.at[w * vp + i, my_pair],
                e_send,
                e_recv,
                to,
                b,
                w,
            )
        return 0

    lax.fori_loop(1, nm, send_e, 0)

    load_c.wait()
    row8 = lax.broadcasted_iota(jnp.int32, (LB, lon), 0)
    first, last = row8 == 0, row8 == LB - 1
    edge = jnp.where(first & up, 1.0, 0.0) + jnp.where(last & down, 1.0, 0.0)
    spilled = []
    for i in range(2):
        f = cbuf[i]
        g = along(f, lon) + KAPPA * (
            jnp.where(first, 0.0, pltpu.roll(f, 1, 0)) + jnp.where(last, 0.0, pltpu.roll(f, LB - 1, 0))
        )
        e1 = KAPPA * f * edge
        sm[i] = along(g, lon) + KAPPA * (
            jnp.where(first, e1, pltpu.roll(g, 1, 0)) + jnp.where(last, e1, pltpu.roll(g, LB - 1, 0))
        )
        spilled.append((along(e1, lon) + KAPPA * g, KAPPA * e1))
    (near0, far0), (near1, far1) = spilled
    packed = jnp.where(row8 == 0, far0, pltpu.roll(near0, 1, 0))
    packed = jnp.where(row8 == 2, pltpu.roll(far1, 2, 0), packed)
    packed = jnp.where(row8 == 3, pltpu.roll(near1, 3, 0), packed)
    packed = jnp.where(row8 == 4, pltpu.roll(near0, 5, 0), packed)
    packed = jnp.where(row8 == 5, pltpu.roll(far0, 6, 0), packed)
    packed = jnp.where(row8 == 6, pltpu.roll(near1, 7, 0), packed)
    packed = jnp.where(row8 == 7, far1, packed)
    s_top[...] = packed[0:4]
    s_bot[...] = packed[4:8]
    s_in[my_pair] = sm[:, :, mine]

    def send_s(k, _):
        to = lax.rem(m + k, nm)
        cut = pl.ds(pl.multiple_of(to * LANES, LANES), LANES)

        @pl.when(k > 0)
        def _():
            start_to(sm.at[:, :, cut], s_in.at[my_pair], s_send.at[0], s_recv.at[0], to, b, w)

        @pl.when(up)
        def _():
            start_to(s_top.at[:, cut], r_bot.at[m], s_send.at[1], s_recv.at[1], to, b - 1, w)

        @pl.when(down)
        def _():
            start_to(s_bot.at[:, cut], r_top.at[m], s_send.at[2], s_recv.at[2], to, b + 1, w)

        return 0

    lax.fori_loop(0, nm, send_s, 0)

    load_d.wait()

    @pl.when(up)
    def _():
        start_to(dif.at[1], dif.at[2], d_send.at[0], d_recv.at[0], m, b - 1, w)

    @pl.when(down)
    def _():
        start_to(dif.at[1], dif.at[0], d_send.at[1], d_recv.at[1], m, b + 1, w)

    @pl.when(jnp.logical_not(up))
    def _():
        dif[0] = jnp.zeros_like(dif[0])
        r_top[...] = jnp.zeros_like(r_top)
        rt[...] = jnp.zeros_like(rt)
        rxt[...] = jnp.zeros_like(rxt)
        c_top[...] = jnp.zeros_like(c_top)
        for it in range(ITERS):
            fstate[it, 0] = jnp.zeros_like(fstate[it, 0])
            bstate[it, 0] = jnp.zeros_like(bstate[it, 0])

    @pl.when(jnp.logical_not(down))
    def _():
        dif[2] = jnp.zeros_like(dif[2])
        r_bot[...] = jnp.zeros_like(r_bot)
        rb[...] = jnp.zeros_like(rb)
        rxb[...] = jnp.zeros_like(rxb)
        c_bot[...] = jnp.zeros_like(c_bot)
        for it in range(ITERS):
            fstate[it, 2] = jnp.zeros_like(fstate[it, 2])
            bstate[it, 2] = jnp.zeros_like(bstate[it, 2])

    @pl.when(jnp.logical_not(before))
    def _():
        ends_prev[...] = jnp.zeros_like(ends_prev)

    @pl.when(jnp.logical_not(after))
    def _():
        inc_next[...] = jnp.zeros_like(inc_next)

    for v in range(NV):
        ewb[v] = jnp.full((LB, LANES), err_w[v], F32)

    tall = lax.broadcasted_iota(jnp.int32, (NV * LB, LANES), 0)
    lane_of = lax.broadcasted_iota(jnp.int32, (LANES, LANES), 0)

    def add_obs(k, total):
        at = pl.ds(k, 1)
        cell = obs_cell[at, :]
        here = (tall == lax.shift_right_logical(cell, 7)) & (obs_window[at, :] == w)
        weight = jnp.where(here, obs_weight[at, :], 0.0)
        both = jnp.concatenate([weight, weight * obs_value[at, :]], axis=0)
        hot = jnp.where(lane_of == (cell & (LANES - 1)), 1.0, 0.0)
        return total + lax.dot_general(
            both,
            hot,
            (((1,), (1,)), ((), ())),
            precision=lax.Precision.HIGHEST,
            preferred_element_type=F32,
        )

    wv[...] = lax.fori_loop(
        0, obs_cell.shape[0], add_obs, jnp.zeros((2 * NV * LB, LANES), F32)
    )

    for i in range(vp):
        drain(et.at[w * vp + i, my_pair], local.at[2])
        drain(et.at[0, pl.ds(0, members - 2)], e_recv)
    start_to(et.at[my_piece], et.at[my_piece], k_send.at[0], k_recv.at[0], m, b, other)
    order = sorted(range(1, planes), key=lambda k: -min(k, planes - k))
    for k in order:
        start_to(
            et.at[my_piece], et.at[my_piece], y_send.at[k], y_recv.at[k], m, b, lax.rem(w + 2 * k, nw)
        )
    for k in reversed(order):
        piece = et.at[pl.ds(lax.rem(w - 2 * k + nw, nw) * vp, vp)]
        drain(piece, y_recv.at[k])
        start_to(piece, piece, k_send.at[k], k_recv.at[k], m, b, other)

    drain(s_in.at[pl.ds(0, members - 2)], s_recv.at[0])

    @pl.when(up)
    def _():
        drain(r_top, s_recv.at[2])

    @pl.when(down)
    def _():
        drain(r_bot, s_recv.at[1])

    def add_spill(q, _):
        for i in range(2):
            j = 2 * q + i
            s_in[j, 0:2] = s_in[j, 0:2] + r_top[q, 2 * i : 2 * i + 2]
            s_in[j, 6:8] = s_in[j, 6:8] + r_bot[q, 2 * i : 2 * i + 2]
        return 0

    lax.fori_loop(0, nm, add_spill, 0)
    for k in range(planes):
        drain(et.at[my_piece], k_recv.at[k])

    rows24 = lax.broadcasted_iota(jnp.int32, (3 * LB, LANES), 0)
    inside24 = ((rows24 >= LB) | up) & ((rows24 < 2 * LB) | down)
    rows16 = lax.broadcasted_iota(jnp.int32, (2 * LB, LANES), 0)
    inside16 = jnp.where(((rows16 >= 4) | up) & ((rows16 < 12) | down), 1.0, 0.0)
    lane16 = lax.broadcasted_iota(jnp.int32, (2 * LB, LANES), 1)
    lane8 = lax.broadcasted_iota(jnp.int32, (LB, LANES), 1)

    def wide(ref):
        return jnp.concatenate([ref[0], ref[1], ref[2]], axis=1)

    def second(x):
        return pltpu.roll(x, 1, 1) + pltpu.roll(x, 3 * LB - 1, 1) - 2.0 * x

    def mixed(x, transposed):
        rows = []
        for v in range(NV):
            total = None
            for u in range(NV):
                term = (coup[u, v] if transposed else coup[v, u]) * x[u]
                total = term if total is None else total + term
            rows.append(total)
        return jnp.stack(rows, axis=0)

    count = jnp.full((3 * LB, LANES), steps[0], jnp.int32)

    def halo(ref, it, which):
        base = 4 * it + 2 * which

        @pl.when(up)
        def _():
            start_to(ref.at[it, 1], ref.at[it, 2], f_send.at[base], f_recv.at[base], m, b - 1, w)

        @pl.when(down)
        def _():
            start_to(ref.at[it, 1], ref.at[it, 0], f_send.at[base + 1], f_recv.at[base + 1], m, b + 1, w)

    def halo_wait(ref, it, which):
        base = 4 * it + 2 * which

        @pl.when(down)
        def _():
            drain(ref.at[it, 2], f_recv.at[base])

        @pl.when(up)
        def _():
            drain(ref.at[it, 0], f_recv.at[base + 1])

    def contract(j, total):
        return total + et[:, j] * s_in[j][None]

    for it in range(ITERS):
        if it == 0:
            total = lax.fori_loop(
                0, members, contract, jnp.zeros((NV, LB, LANES), F32), unroll=4
            )
            fstate[it, 1] = total * scale

            @pl.when(up)
            def _():
                drain(dif.at[0], d_recv.at[1])

            @pl.when(down)
            def _():
                drain(dif.at[2], d_recv.at[0])
        else:
            pfull[:, 4:12] = rx[...]
            pfull[:, 0:4] = rxt[...]
            pfull[:, 12:16] = rxb[...]

            def place(j, _):
                ext[j, 0:4] = rt[j]
                ext[j, 12:16] = rb[j]
                return 0

            lax.fori_loop(0, members, place, 0, unroll=4)

            def twice(g, total):
                f0 = ext[pl.ds(GROUP * g, GROUP)]
                sides = []
                for i in range(GROUP):
                    j = GROUP * g + i
                    from_right = pltpu.roll(pfull[1], lax.rem(LANES - 4 * j, LANES), 1)
                    from_left = pltpu.roll(pfull[0], LANES - 4 - 4 * j, 1)
                    sides.append(
                        jnp.where(lane16 < 4, from_right, jnp.where(lane16 >= LANES - 4, from_left, 0.0))
                    )
                f1 = jnp.stack(sides, axis=0)
                for _ in range(4):
                    fl0, fl1 = pltpu.roll(f0, 1, 2), pltpu.roll(f1, 1, 2)
                    fr0, fr1 = pltpu.roll(f0, LANES - 1, 2), pltpu.roll(f1, LANES - 1, 2)
                    start, end = lane16 == 0, lane16 == LANES - 1
                    n0 = (
                        jnp.where(start, fl1, fl0)
                        + jnp.where(end, fr1, fr0)
                        + pltpu.roll(f0, 1, 1)
                        + pltpu.roll(f0, 2 * LB - 1, 1)
                    )
                    n1 = (
                        jnp.where(start, fl0, fl1)
                        + jnp.where(end, fr0, fr1)
                        + pltpu.roll(f1, 1, 1)
                        + pltpu.roll(f1, 2 * LB - 1, 1)
                    )
                    f0 = (CENTER * f0 + KAPPA * n0) * inside16
                    f1 = (CENTER * f1 + KAPPA * n1) * inside16
                sq[...] = f0
                for i in range(GROUP):
                    total = total + et[:, GROUP * g + i] * sq[i, 4:12][None]
                return total

            total = lax.fori_loop(
                0, members // GROUP, twice, jnp.zeros((NV, LB, LANES), F32)
            )
            fstate[it, 1] = KEEP * fstate[it - 1, 1] - (DESCENT * scale) * total

        halo(fstate, it, 0)

        @pl.when(before)
        def _():
            start_to(
                fstate.at[it, 1], inc_next.at[it], w_send.at[2 * it], w_recv.at[2 * it], m, b, w - 1
            )

        if it == ITERS - 1:
            store_inc = pltpu.make_async_copy(fstate.at[it, 1], inc_out.at[0], local.at[3])
            store_inc.start()
        halo_wait(fstate, it, 0)
        coeff = wide(dif)

        def forth(k, u):
            moved = u + coeff * second(u) + mixed(u, False)
            moved = jnp.where(inside24, moved, 0.0)
            return jnp.where(k < count, moved, u)

        state = lax.fori_loop(0, KMAX, forth, wide(fstate.at[it]))
        ends = state[:, LB : 2 * LB]
        ends_own[it] = ends

        @pl.when(after)
        def _():
            start_to(
                ends_own.at[it],
                ends_prev.at[it],
                w_send.at[2 * it + 1],
                w_recv.at[2 * it + 1],
                m,
                b,
                w + 1,
            )

        @pl.when(after)
        def _():
            drain(inc_next.at[it], w_recv.at[2 * it])

        dense = wv[...].reshape(2, NV, LB, LANES)
        to_next = jnp.where(after, ewb[...] * (ends - inc_next[it]), 0.0)
        bstate[it, 1] = dense[0] * ends - dense[1] + to_next
        halo(bstate, it, 1)
        halo_wait(bstate, it, 1)

        def back(k, y):
            moved = y + second(coeff * y) + mixed(y, True)
            moved = jnp.where(inside24, moved, 0.0)
            return jnp.where(KMAX - 1 - k < count, moved, y)

        state = lax.fori_loop(0, KMAX, back, wide(bstate.at[it]))

        @pl.when(before)
        def _():
            drain(ends_prev.at[it], w_recv.at[2 * it + 1])

        misfit = jnp.where(before, ewb[...] * (ends_prev[it] - fstate[it, 1]), 0.0)
        gradient = (state[:, LB : 2 * LB] - misfit) * scale

        if it == 0:

            def spread(j, carry):
                lo, hi = carry
                x = jnp.sum(et[:, j] * gradient, axis=0)
                b1[j] = x
                ext[j, 4:12] = x
                ts[j] = x[0:4]
                bs[j] = x[4:8]
                here = lax.shift_right_logical(lane8, 2) == j
                lo = jnp.where(here, pltpu.roll(x, 4 * j, 1), lo)
                hi = jnp.where(here, pltpu.roll(x, lax.rem(4 * j + 4, LANES), 1), hi)
                return lo, hi

            blank = jnp.zeros((LB, LANES), F32)
            lo, hi = lax.fori_loop(0, members, spread, (blank, blank), unroll=4)
            for side, value in enumerate((lo, hi)):
                pk[side] = value
                pkt[side] = value[0:4]
                pkb[side] = value[4:8]

            @pl.when(up)
            def _():
                start_to(ts, rb, h_send.at[0], h_recv.at[0], m, b - 1, w)
                start_to(pkt.at[0], rxb.at[1], h_send.at[2], h_recv.at[2], left, b - 1, w)
                start_to(pkt.at[1], rxb.at[0], h_send.at[3], h_recv.at[3], right, b - 1, w)

            @pl.when(down)
            def _():
                start_to(bs, rt, h_send.at[1], h_recv.at[1], m, b + 1, w)
                start_to(pkb.at[0], rxt.at[1], h_send.at[4], h_recv.at[4], left, b + 1, w)
                start_to(pkb.at[1], rxt.at[0], h_send.at[5], h_recv.at[5], right, b + 1, w)

            start_to(pk.at[0], rx.at[1], h_send.at[6], h_recv.at[6], left, b, w)
            start_to(pk.at[1], rx.at[0], h_send.at[7], h_recv.at[7], right, b, w)
            drain(rx.at[1], h_recv.at[6])
            drain(rx.at[0], h_recv.at[7])

            @pl.when(down)
            def _():
                drain(rb, h_recv.at[0])
                drain(rxb.at[1], h_recv.at[2])
                drain(rxb.at[0], h_recv.at[3])

            @pl.when(up)
            def _():
                drain(rt, h_recv.at[1])
                drain(rxt.at[1], h_recv.at[4])
                drain(rxt.at[0], h_recv.at[5])
        else:

            def gather(q, _):
                for i in range(2):
                    j = 2 * q + i
                    x = jnp.sum(et[:, j] * gradient, axis=0)
                    x = (KEEP * DESCENT) * b1[j] + DESCENT * x
                    bsum[j] = x
                    o_top[q, 2 * i : 2 * i + 2] = x[0:2]
                    o_bot[q, 2 * i : 2 * i + 2] = x[6:8]
                return 0

            lax.fori_loop(0, nm, gather, 0)

    c_in[:, :, mine] = bsum[my_pair]

    def send_o(k, _):
        to = lax.rem(m + k, nm)

        @pl.when(k > 0)
        def _():
            start_to(
                bsum.at[pl.ds(2 * to, 2)], c_in.at[:, :, mine], o_send.at[0], o_recv.at[0], to, b, w
            )

        @pl.when(up)
        def _():
            start_to(o_top.at[to], c_bot.at[:, mine], o_send.at[1], o_recv.at[1], to, b - 1, w)

        @pl.when(down)
        def _():
            start_to(o_bot.at[to], c_top.at[:, mine], o_send.at[2], o_recv.at[2], to, b + 1, w)

        return 0

    lax.fori_loop(0, nm, send_o, 0)
    drain(bsum.at[pl.ds(0, members - 2)], s_send.at[0])
    drain(bsum.at[pl.ds(0, members - 2)], o_recv.at[0])

    @pl.when(down)
    def _():
        drain(s_bot, s_send.at[2])
        drain(c_bot, o_recv.at[1])

    @pl.when(up)
    def _():
        drain(s_top, s_send.at[1])
        drain(c_top, o_recv.at[2])

    packed = jnp.concatenate([c_top[...], c_bot[...]], axis=0)
    for i in range(2):
        f = c_in[i]
        near = jnp.where(
            first,
            pltpu.roll(packed, LB - (2 * i + 1), 0),
            pltpu.roll(packed, 3 - 2 * i, 0),
        )
        far = jnp.where(
            first,
            pltpu.roll(packed, (LB - 2 * i) % LB, 0) if i else packed,
            pltpu.roll(packed, 2 - 2 * i, 0) if i == 0 else packed,
        )
        g = along(f, lon) + KAPPA * (
            jnp.where(first, near, pltpu.roll(f, 1, 0)) + jnp.where(last, near, pltpu.roll(f, LB - 1, 0))
        )
        e1 = (along(near, lon) + KAPPA * (far + f)) * edge
        h = along(g, lon) + KAPPA * (
            jnp.where(first, e1, pltpu.roll(g, 1, 0)) + jnp.where(last, e1, pltpu.roll(g, LB - 1, 0))
        )
        sm[i] = (KEEP * KEEP) * cbuf[i] - h
    store_c = pltpu.make_async_copy(sm, ctl_out.at[0], local.at[4])
    store_c.start()

    for i in range(vp):
        drain(et.at[0, pl.ds(0, members - 2)], e_send)
    for k in range(planes):
        drain(et.at[my_piece], k_send.at[k])
        if k > 0:
            drain(et.at[my_piece], y_send.at[k])
    drain(bsum.at[pl.ds(0, members - 2)], o_send.at[0])

    @pl.when(up)
    def _():
        drain(dif.at[1], d_send.at[0])
        drain(o_top, o_send.at[1])
        drain(ts, h_send.at[0])
        drain(pkt.at[0], h_send.at[2])
        drain(pkt.at[1], h_send.at[3])
        for it in range(ITERS):
            drain(fstate.at[it, 1], f_send.at[4 * it])
            drain(bstate.at[it, 1], f_send.at[4 * it + 2])

    @pl.when(down)
    def _():
        drain(dif.at[1], d_send.at[1])
        drain(o_bot, o_send.at[2])
        drain(bs, h_send.at[1])
        drain(pkb.at[0], h_send.at[4])
        drain(pkb.at[1], h_send.at[5])
        for it in range(ITERS):
            drain(fstate.at[it, 1], f_send.at[4 * it + 1])
            drain(bstate.at[it, 1], f_send.at[4 * it + 3])

    drain(pk.at[0], h_send.at[6])
    drain(pk.at[1], h_send.at[7])
    for it in range(ITERS):

        @pl.when(before)
        def _():
            drain(fstate.at[it, 1], w_send.at[2 * it])

        @pl.when(after)
        def _():
            drain(ends_own.at[it], w_send.at[2 * it + 1])

    store_inc.wait()
    store_c.wait()


def local_part(nm, nl, nw, *args):
    (
        ensemble,
        weights,
        diffusivity,
        coupling,
        tl_steps,
        obs_cell,
        obs_window,
        obs_value,
        obs_weight,
        error_weight,
    ) = args
    members = 2 * nm
    lon = nm * LANES
    planes = nw // 2
    anywhere = pl.BlockSpec(memory_space=pl.ANY)
    vmem = pl.BlockSpec(memory_space=pltpu.VMEM)
    smem = pl.BlockSpec(memory_space=pltpu.SMEM)
    obs = [x.reshape(-1, LANES) for x in (obs_cell, obs_window, obs_value, obs_weight)]
    tile = (LB, LANES)
    state = (NV, *tile)
    half = (4, LANES)

    def buf(*shape):
        return pltpu.VMEM(shape, F32)

    dma = pltpu.SemaphoreType.DMA
    return pl.pallas_call(
        functools.partial(kernel, nm, nl, nw),
        name="assimilate",
        out_shape=(
            jax.ShapeDtypeStruct((1, 2, LB, lon), F32),
            jax.ShapeDtypeStruct((1, *state), F32),
        ),
        in_specs=[anywhere, anywhere, anywhere, smem, smem, vmem, vmem, vmem, vmem, smem],
        out_specs=(anywhere, anywhere),
        scratch_shapes=[
            buf(NV, members, *tile),
            buf(2, LB, lon),
            buf(2, LB, lon),
            buf(4, lon),
            buf(4, lon),
            buf(members, *tile),
            buf(nm, *half),
            buf(nm, *half),
            buf(3, *state),
            buf(ITERS, 3, *state),
            buf(ITERS, 3, *state),
            buf(ITERS, *state),
            buf(ITERS, *state),
            buf(ITERS, *state),
            buf(2 * NV * LB, LANES),
            buf(*state),
            buf(members, *tile),
            buf(members, *half),
            buf(members, *half),
            buf(members, *half),
            buf(members, *half),
            buf(2, *tile),
            buf(2, *half),
            buf(2, *half),
            buf(2, *tile),
            buf(2, *half),
            buf(2, *half),
            buf(2, 2 * LB, LANES),
            buf(members, 2 * LB, LANES),
            buf(GROUP, 2 * LB, LANES),
            buf(members, *tile),
            buf(nm, *half),
            buf(nm, *half),
            buf(2, LB, lon),
            buf(4, lon),
            buf(4, lon),
            dma((5,)),
            dma,
            dma,
            dma((planes,)),
            dma((planes,)),
            dma((planes,)),
            dma((planes,)),
            dma((3,)),
            dma((3,)),
            dma((2,)),
            dma((2,)),
            dma((4 * ITERS,)),
            dma((4 * ITERS,)),
            dma((2 * ITERS,)),
            dma((2 * ITERS,)),
            dma((8,)),
            dma((8,)),
            dma((3,)),
            dma((3,)),
        ],
        compiler_params=pltpu.CompilerParams(
            collective_id=0, has_side_effects=True, vmem_limit_bytes=40 * 1024 * 1024
        ),
    )(
        ensemble,
        weights,
        diffusivity,
        coupling,
        tl_steps,
        *obs,
        error_weight,
    )


def solution(mesh):
    sizes = [mesh.shape[axis] for axis in ("mem", "lat", "win")]
    return jax.shard_map(
        functools.partial(local_part, *sizes),
        mesh=mesh,
        in_specs=(
            P("mem", None, "lat", None),
            P("win", "mem", "lat", None),
            P(None, "lat", "mem"),
            P(),
            P("win"),
            P(("mem", "lat")),
            P(("mem", "lat")),
            P(("mem", "lat")),
            P(("mem", "lat")),
            P(),
        ),
        out_specs=(P("win", "mem", "lat", None), P("win", None, "lat", "mem")),
        check_vma=False,
    )
```

```python
import functools
import math

import jax
import jax.numpy as jnp
from jax import lax
from jax.experimental import pallas as pl
from jax.experimental.pallas import tpu as pltpu
from jax.sharding import PartitionSpec as P

MESH = pl.DeviceIdType.MESH
NV = 8
LB = 8
LANES = 128
KMAX = 6
ITERS = 2
KAPPA = 0.125
DESCENT = 0.25
KEEP = 1.0 - DESCENT
CENTER = 1.0 - 4.0 * KAPPA
F32 = jnp.float32


def start_to(src, dst, send_sem, recv_sem, mem, lat, win):
    pltpu.make_async_remote_copy(
        src_ref=src,
        dst_ref=dst,
        send_sem=send_sem,
        recv_sem=recv_sem,
        device_id={"mem": mem, "lat": lat, "win": win},
        device_id_type=MESH,
    ).start()


def drain(ref, sem):
    pltpu.make_async_copy(ref, ref, sem).wait()


def along(f, lon):
    return CENTER * f + KAPPA * (pltpu.roll(f, 1, 1) + pltpu.roll(f, lon - 1, 1))


def kernel(
    nm,
    nl,
    nw,
    e_hbm,
    c_hbm,
    d_hbm,
    coup_hbm,
    steps,
    obs0,
    obs1,
    obs2,
    obs3,
    err_hbm,
    ctl_out,
    inc_out,
    coup,
    err_w,
    obs_cell,
    obs_window,
    obs_value,
    obs_weight,
    et,
    cbuf,
    sm,
    s_top,
    s_bot,
    s_in,
    r_top,
    r_bot,
    dif,
    fstate,
    bstate,
    inc_next,
    ends_own,
    ends_prev,
    wv,
    ewb,
    e_up,
    e_down,
    eh,
    b1,
    bh,
    b_up,
    b_down,
    r_far,
    pk,
    rx,
    rxc,
    sq,
    obuf,
    c_in,
    local,
    e_send,
    e_recv,
    y_send,
    y_recv,
    k_send,
    k_recv,
    s_send,
    s_recv,
    d_send,
    d_recv,
    f_send,
    f_recv,
    w_send,
    w_recv,
    g_send,
    g_recv,
    y2_send,
    y2_recv,
    k2_send,
    k2_recv,
    h_send,
    h_recv,
    o_send,
    o_recv,
):
    m, b, w = lax.axis_index("mem"), lax.axis_index("lat"), lax.axis_index("win")
    members = 2 * nm
    lon = nm * LANES
    vp = NV // nw
    scale = 1.0 / math.sqrt(members - 1)
    up, down = b > 0, b < nl - 1
    before, after = w > 0, w < nw - 1
    other = w + 1 - 2 * lax.rem(w, 2)
    planes = nw // 2
    groups = members // LB
    left, right = lax.rem(m + nm - 1, nm), lax.rem(m + 1, nm)
    mine = pl.ds(pl.multiple_of(m * LANES, LANES), LANES)
    my_pair = pl.ds(2 * m, 2)
    my_piece = pl.ds(w * vp, vp)

    load_c = pltpu.make_async_copy(c_hbm.at[0], cbuf, local.at[0])
    load_c.start()
    load_d = pltpu.make_async_copy(d_hbm, dif.at[1], local.at[1])
    load_d.start()
    small = [
        pltpu.make_async_copy(src, dst, local.at[5 + i])
        for i, (src, dst) in enumerate(
            (
                (coup_hbm, coup),
                (err_hbm, err_w),
                (obs0, obs_cell),
                (obs1, obs_window),
                (obs2, obs_value),
                (obs3, obs_weight),
            )
        )
    ]
    for copy in small:
        copy.start()
    for i in range(vp):
        pltpu.make_async_copy(
            e_hbm.at[:, w * vp + i, :, mine], et.at[w * vp + i, my_pair], local.at[2]
        ).start()

    barrier = pltpu.get_barrier_semaphore()

    def hello(mem, lat, win):
        pl.semaphore_signal(
            barrier, inc=1, device_id={"mem": mem, "lat": lat, "win": win}, device_id_type=MESH
        )

    def greet(k, _):
        to = lax.rem(m + k, nm)

        @pl.when(k > 0)
        def _():
            hello(to, b, w)

        @pl.when(up)
        def _():
            hello(to, b - 1, w)

        @pl.when(down)
        def _():
            hello(to, b + 1, w)

        return 0

    lax.fori_loop(0, nm, greet, 0)
    for k in range(1, planes):
        hello(m, b, lax.rem(w + 2 * k, nw))
    hello(m, b, other)
    odd = lax.rem(w, 2)

    @pl.when((odd == 0) & before)
    def _():
        hello(m, b, w - 1)

    @pl.when((odd == 1) & after)
    def _():
        hello(m, b, w + 1)

    one_more = jnp.where((w > 0) & (w < nw - 1), 1, 0)
    bands = jnp.where(up, 1, 0) + jnp.where(down, 1, 0)
    pl.semaphore_wait(barrier, nm - 1 + nm * bands + planes + one_more)

    def send_e(k, _):
        to = lax.rem(m + k, nm)
        for i in range(vp):
            start_to(
                e_hbm.at[:, w * vp + i, :, pl.ds(pl.multiple_of(to * LANES, LANES), LANES)],
                et.at[w * vp + i, my_pair],
                e_send,
                e_recv,
                to,
                b,
                w,
            )
        return 0

    lax.fori_loop(1, nm, send_e, 0)

    load_c.wait()
    row8 = lax.broadcasted_iota(jnp.int32, (LB, lon), 0)
    first, last = row8 == 0, row8 == LB - 1
    edge = jnp.where(first & up, 1.0, 0.0) + jnp.where(last & down, 1.0, 0.0)
    spilled = []
    for i in range(2):
        f = cbuf[i]
        g = along(f, lon) + KAPPA * (
            jnp.where(first, 0.0, pltpu.roll(f, 1, 0)) + jnp.where(last, 0.0, pltpu.roll(f, LB - 1, 0))
        )
        e1 = KAPPA * f * edge
        sm[i] = along(g, lon) + KAPPA * (
            jnp.where(first, e1, pltpu.roll(g, 1, 0)) + jnp.where(last, e1, pltpu.roll(g, LB - 1, 0))
        )
        spilled.append((along(e1, lon) + KAPPA * g, KAPPA * e1))
    (near0, far0), (near1, far1) = spilled
    packed = jnp.where(row8 == 0, far0, pltpu.roll(near0, 1, 0))
    packed = jnp.where(row8 == 2, pltpu.roll(far1, 2, 0), packed)
    packed = jnp.where(row8 == 3, pltpu.roll(near1, 3, 0), packed)
    packed = jnp.where(row8 == 4, pltpu.roll(near0, 5, 0), packed)
    packed = jnp.where(row8 == 5, pltpu.roll(far0, 6, 0), packed)
    packed = jnp.where(row8 == 6, pltpu.roll(near1, 7, 0), packed)
    packed = jnp.where(row8 == 7, far1, packed)
    s_top[...] = packed[0:4]
    s_bot[...] = packed[4:8]
    s_in[my_pair] = sm[:, :, mine]

    def send_s(k, _):
        to = lax.rem(m + k, nm)
        cut = pl.ds(pl.multiple_of(to * LANES, LANES), LANES)

        @pl.when(up)
        def _():
            start_to(s_top.at[:, cut], r_bot.at[m], s_send.at[1], s_recv.at[1], to, b - 1, w)

        @pl.when(down)
        def _():
            start_to(s_bot.at[:, cut], r_top.at[m], s_send.at[2], s_recv.at[2], to, b + 1, w)

        return 0

    def send_s_own(k, _):
        to = lax.rem(m + k, nm)
        cut = pl.ds(pl.multiple_of(to * LANES, LANES), LANES)
        start_to(sm.at[:, :, cut], s_in.at[my_pair], s_send.at[0], s_recv.at[0], to, b, w)
        return 0

    lax.fori_loop(0, nm, send_s, 0)
    lax.fori_loop(1, nm, send_s_own, 0)

    @pl.when(jnp.logical_not(up))
    def _():
        dif[0] = jnp.zeros_like(dif[0])
        r_top[...] = jnp.zeros_like(r_top)
        r_far[0] = jnp.zeros_like(r_far[0])
        rxc[0] = jnp.zeros_like(rxc[0])
        for i in range(vp):
            eh[w * vp + i, 0] = jnp.zeros_like(r_far[0])
        for it in range(ITERS):
            fstate[it, 0] = jnp.zeros_like(fstate[it, 0])
            bstate[it, 0] = jnp.zeros_like(bstate[it, 0])

    @pl.when(jnp.logical_not(down))
    def _():
        dif[2] = jnp.zeros_like(dif[2])
        r_bot[...] = jnp.zeros_like(r_bot)
        r_far[1] = jnp.zeros_like(r_far[1])
        rxc[1] = jnp.zeros_like(rxc[1])
        for i in range(vp):
            eh[w * vp + i, 1] = jnp.zeros_like(r_far[1])
        for it in range(ITERS):
            fstate[it, 2] = jnp.zeros_like(fstate[it, 2])
            bstate[it, 2] = jnp.zeros_like(bstate[it, 2])

    @pl.when(jnp.logical_not(before))
    def _():
        ends_prev[...] = jnp.zeros_like(ends_prev)

    @pl.when(jnp.logical_not(after))
    def _():
        inc_next[...] = jnp.zeros_like(inc_next)

    for copy in small:
        copy.wait()
    for v in range(NV):
        ewb[v] = jnp.full((LB, LANES), err_w[v], F32)

    tall = lax.broadcasted_iota(jnp.int32, (NV * LB, LANES), 0)
    lane_of = lax.broadcasted_iota(jnp.int32, (LANES, LANES), 0)

    def add_obs(k, total):
        at = pl.ds(k, 1)
        cell = obs_cell[at, :]
        here = (tall == lax.shift_right_logical(cell, 7)) & (obs_window[at, :] == w)
        weight = jnp.where(here, obs_weight[at, :], 0.0)
        both = jnp.concatenate([weight, weight * obs_value[at, :]], axis=0)
        hot = jnp.where(lane_of == (cell & (LANES - 1)), 1.0, 0.0)
        return total + lax.dot_general(
            both,
            hot,
            (((1,), (1,)), ((), ())),
            precision=lax.Precision.HIGHEST,
            preferred_element_type=F32,
        )

    wv[...] = lax.fori_loop(
        0, obs_cell.shape[0], add_obs, jnp.zeros((2 * NV * LB, LANES), F32)
    )

    for i in range(vp):
        drain(et.at[w * vp + i, my_pair], local.at[2])
        drain(et.at[0, pl.ds(0, members - 2)], e_recv)
    start_to(et.at[my_piece], et.at[my_piece], k_send.at[0], k_recv.at[0], m, b, other)
    order = sorted(range(1, planes), key=lambda k: -min(k, planes - k))
    for k in order:
        start_to(
            et.at[my_piece], et.at[my_piece], y_send.at[k], y_recv.at[k], m, b, lax.rem(w + 2 * k, nw)
        )
    drain(s_in.at[pl.ds(0, members - 2)], s_recv.at[0])

    @pl.when(up)
    def _():
        drain(r_top, s_recv.at[2])

    @pl.when(down)
    def _():
        drain(r_bot, s_recv.at[1])

    def add_spill(q, _):
        for i in range(2):
            j = 2 * q + i
            s_in[j, 0:2] = s_in[j, 0:2] + r_top[q, 2 * i : 2 * i + 2]
            s_in[j, 6:8] = s_in[j, 6:8] + r_bot[q, 2 * i : 2 * i + 2]
        return 0

    lax.fori_loop(0, nm, add_spill, 0)
    load_d.wait()

    @pl.when(up)
    def _():
        start_to(dif.at[1], dif.at[2], d_send.at[0], d_recv.at[0], m, b - 1, w)

    @pl.when(down)
    def _():
        start_to(dif.at[1], dif.at[0], d_send.at[1], d_recv.at[1], m, b + 1, w)

    def first_increment(v):
        fstate[0, 1, v] = jnp.sum(et[v] * s_in[...], axis=0) * scale

    for i in range(vp):
        v = w * vp + i
        for j in range(members):
            e_up[2 * j : 2 * j + 2, :] = et[v, j, 0:2]
            e_down[2 * j : 2 * j + 2, :] = et[v, j, 6:8]

        @pl.when(up)
        def _():
            start_to(e_up, eh.at[v, 1], g_send.at[0], g_recv.at[0], m, b - 1, w)

        @pl.when(down)
        def _():
            start_to(e_down, eh.at[v, 0], g_send.at[1], g_recv.at[1], m, b + 1, w)

        if i < vp - 1:

            @pl.when(up)
            def _():
                drain(e_up, g_send.at[0])

            @pl.when(down)
            def _():
                drain(e_down, g_send.at[1])

        first_increment(v)

    for k in reversed(order):
        origin = lax.rem(w - 2 * k + nw, nw) * vp
        piece = et.at[pl.ds(origin, vp)]
        drain(piece, y_recv.at[k])
        start_to(piece, piece, k_send.at[k], k_recv.at[k], m, b, other)
        for i in range(vp):
            first_increment(origin + i)
    for k in [0, *reversed(order)]:
        origin = lax.rem(other - 2 * k + nw, nw) * vp
        drain(et.at[pl.ds(origin, vp)], k_recv.at[k])
        for i in range(vp):
            first_increment(origin + i)

    rows24 = lax.broadcasted_iota(jnp.int32, (3 * LB, LANES), 0)
    inside24 = ((rows24 >= LB) | up) & ((rows24 < 2 * LB) | down)
    lane = lax.broadcasted_iota(jnp.int32, (LB, LANES), 1)
    row = lax.broadcasted_iota(jnp.int32, (LB, LANES), 0)
    up_f = jnp.where(up, 1.0, 0.0)
    down_f = jnp.where(down, 1.0, 0.0)

    def wide(ref):
        return jnp.concatenate([ref[0], ref[1], ref[2]], axis=1)

    def second(x):
        return pltpu.roll(x, 1, 1) + pltpu.roll(x, 3 * LB - 1, 1) - 2.0 * x

    def mixed(x, transposed):
        rows = []
        for v in range(NV):
            total = None
            for u in range(NV):
                term = (coup[u, v] if transposed else coup[v, u]) * x[u]
                total = term if total is None else total + term
            rows.append(total)
        return jnp.stack(rows, axis=0)

    count = jnp.full((3 * LB, LANES), steps[0], jnp.int32)

    def halo(ref, it, which):
        base = 4 * it + 2 * which

        @pl.when(up)
        def _():
            start_to(ref.at[it, 1], ref.at[it, 2], f_send.at[base], f_recv.at[base], m, b - 1, w)

        @pl.when(down)
        def _():
            start_to(ref.at[it, 1], ref.at[it, 0], f_send.at[base + 1], f_recv.at[base + 1], m, b + 1, w)

    def halo_wait(ref, it, which):
        base = 4 * it + 2 * which

        @pl.when(down)
        def _():
            drain(ref.at[it, 2], f_recv.at[base])

        @pl.when(up)
        def _():
            drain(ref.at[it, 0], f_recv.at[base + 1])

    my_edges = eh.at[my_piece]

    def send_edges():
        for i in range(vp):

            @pl.when(down)
            def _():
                drain(eh.at[0, 1], g_recv.at[0])

            @pl.when(up)
            def _():
                drain(eh.at[0, 0], g_recv.at[1])

        start_to(my_edges, my_edges, k2_send.at[0], k2_recv.at[0], m, b, other)
        for k in order:
            start_to(my_edges, my_edges, y2_send.at[k], y2_recv.at[k], m, b, lax.rem(w + 2 * k, nw))

    def pass_edges():
        for k in reversed(order):
            piece = eh.at[pl.ds(lax.rem(w - 2 * k + nw, nw) * vp, vp)]
            drain(piece, y2_recv.at[k])
            start_to(piece, piece, k2_send.at[k], k2_recv.at[k], m, b, other)

    def rows_of(ref, first_row, stride, g):
        return ref[pl.ds(g * LB * stride + first_row, LB, stride=stride), :]

    def beside(x, y, to_left):
        shift, end = (1, lane == 0) if to_left else (LANES - 1, lane == LANES - 1)
        return jnp.where(end, pltpu.roll(y, shift, 2), pltpu.roll(x, shift, 2))

    def masked(x, depth):
        n = x.shape[0]
        return jnp.concatenate([x[:depth] * up_f, x[depth : n - depth], x[n - depth :] * down_f], axis=0)

    def smooth_group(g):
        main = [r_far[0, pl.ds(2 * LB * g + r, LB, stride=2), :] for r in range(2)]
        main += [bh[0, pl.ds(2 * LB * g + r, LB, stride=2), :] for r in range(2)]
        main += [rows_of(b1, r, LB, g) for r in range(LB)]
        main += [bh[1, pl.ds(2 * LB * g + r, LB, stride=2), :] for r in range(2)]
        main += [r_far[1, pl.ds(2 * LB * g + r, LB, stride=2), :] for r in range(2)]
        places = [(rxc, 0, 4), (rxc, 0, 5), (rx, 1, 0), (rx, 1, 1)]
        places += [(rx, 0, r) for r in range(LB)]
        places += [(rx, 1, 2), (rx, 1, 3), (rxc, 1, 2), (rxc, 1, 3)]
        sides = []
        for ref, which, r in places:
            at = 4 * (groups * r + g)
            lo, hi = (ref[which, 0], ref[which, 1]) if ref is rxc else (ref[0, which], ref[1, which])
            from_left = pltpu.roll(lo, LANES - 4 - at, 1)
            from_right = pltpu.roll(hi, (LANES - at) % LANES, 1)
            sides.append(jnp.where(lane < 4, from_right, jnp.where(lane >= LANES - 4, from_left, 0.0)))
        f0, f1 = jnp.stack(main, axis=0), jnp.stack(sides, axis=0)
        for depth in (3, 2, 1, 0):
            m0, m1 = f0[1:-1], f1[1:-1]
            n0 = beside(m0, m1, True) + beside(m0, m1, False) + f0[2:] + f0[:-2]
            n1 = beside(m1, m0, True) + beside(m1, m0, False) + f1[2:] + f1[:-2]
            f0 = CENTER * m0 + KAPPA * n0
            f1 = CENTER * m1 + KAPPA * n1
            if depth:
                f0, f1 = masked(f0, depth), masked(f1, depth)
        for r in range(LB):
            sq[pl.ds(LB * LB * g + r, LB, stride=LB), :] = f0[r]

    def member_rows(j):
        return pl.ds(pl.multiple_of(LB * j, LB), LB)

    def fourfold(x, from_row):
        x = jnp.where((row == from_row) | (row == from_row + 1), x, 0.0)
        x = x + pltpu.roll(x, 2, 1)
        return x + pltpu.roll(x, 4, 1)

    def edge_rows(gradient):
        out = []
        for side, part in enumerate((gradient[:, :LB], gradient[:, 2 * LB :])):
            tile = fourfold(part, 0 if side else LB - 2)
            rows = eh[:, side].reshape(NV, groups * 2, LB, LANES)
            out.append(jnp.sum(rows * tile[:, None], axis=0).reshape(2 * members, LANES))
        return out

    for it in range(ITERS):
        if it > 0:
            total = jnp.zeros((NV, LB, LANES), F32)
            drain(rx.at[1], h_recv.at[0])
            drain(rx.at[0], h_recv.at[1])

            @pl.when(down)
            def _():
                drain(rxc.at[1, 1], h_recv.at[2])
                drain(rxc.at[1, 0], h_recv.at[3])

            @pl.when(up)
            def _():
                drain(rxc.at[0, 1], h_recv.at[4])
                drain(rxc.at[0, 0], h_recv.at[5])

            def add_member(j, total):
                return total + et[:, j] * sq[member_rows(j), :][None]

            for g in range(groups):
                part = pl.ds(2 * LB * g, 2 * LB)

                @pl.when(down)
                def _():
                    drain(r_far.at[1, part], h_recv.at[6 + 2 * g])

                @pl.when(up)
                def _():
                    drain(r_far.at[0, part], h_recv.at[7 + 2 * g])

                smooth_group(g)
                total = lax.fori_loop(LB * g, LB * (g + 1), add_member, total, unroll=True)
            fstate[it, 1] = KEEP * fstate[it - 1, 1] - (DESCENT * scale) * total

        halo(fstate, it, 0)

        @pl.when(before)
        def _():
            start_to(
                fstate.at[it, 1], inc_next.at[it], w_send.at[2 * it], w_recv.at[2 * it], m, b, w - 1
            )

        if it == ITERS - 1:
            inc_out[0] = fstate[it, 1]
        else:
            send_edges()

            @pl.when(up)
            def _():
                drain(dif.at[0], d_recv.at[1])

            @pl.when(down)
            def _():
                drain(dif.at[2], d_recv.at[0])

        halo_wait(fstate, it, 0)
        coeff = wide(dif)

        def forth(k, u):
            moved = u + coeff * second(u) + mixed(u, False)
            moved = jnp.where(inside24, moved, 0.0)
            return jnp.where(k < count, moved, u)

        state = lax.fori_loop(0, KMAX, forth, wide(fstate.at[it]))
        ends = state[:, LB : 2 * LB]
        for part in range(3):
            ends_own[it, part] = state[:, LB * part : LB * (part + 1)]

        @pl.when(after)
        def _():
            start_to(
                ends_own.at[it],
                ends_prev.at[it],
                w_send.at[2 * it + 1],
                w_recv.at[2 * it + 1],
                m,
                b,
                w + 1,
            )

        @pl.when(after)
        def _():
            drain(inc_next.at[it], w_recv.at[2 * it])

        dense = wv[...].reshape(2, NV, LB, LANES)
        to_next = jnp.where(after, ewb[...] * (ends - inc_next[it]), 0.0)
        bstate[it, 1] = dense[0] * ends - dense[1] + to_next
        halo(bstate, it, 1)
        if it == 0:
            pass_edges()
        halo_wait(bstate, it, 1)

        def back(k, y):
            moved = y + second(coeff * y) + mixed(y, True)
            moved = jnp.where(inside24, moved, 0.0)
            return jnp.where(KMAX - 1 - k < count, moved, y)

        state = lax.fori_loop(0, KMAX, back, wide(bstate.at[it]))

        @pl.when(before)
        def _():
            drain(ends_prev.at[it], w_recv.at[2 * it + 1])

        wide_w = jnp.concatenate([ewb[...]] * 3, axis=1)
        misfit = jnp.where(before, wide_w * (wide(ends_prev.at[it]) - wide(fstate.at[it])), 0.0)
        gradient = (state - misfit) * scale
        own = gradient[:, LB : 2 * LB]

        if it == 0:

            def spread(j, _):
                b1[member_rows(j), :] = jnp.sum(et[:, j] * own, axis=0)
                return 0

            lax.fori_loop(0, members, spread, 0, unroll=4)
            for g in range(groups):
                for r in range(2):
                    to_row = pl.ds(2 * LB * g + r, LB, stride=2)
                    b_up[to_row, :] = rows_of(b1, 2 + r, LB, g)
                    b_down[to_row, :] = rows_of(b1, 4 + r, LB, g)

            for k in range(planes):
                drain(my_edges, k2_recv.at[k])
            top, bottom = edge_rows(gradient)
            bh[0] = top
            bh[1] = bottom
            for part in range(2):
                lo = hi = jnp.zeros((LB, LANES), F32)
                for r in range(LB if part == 0 else 4):
                    for g in range(groups):
                        if part == 0:
                            x = rows_of(b1, r, LB, g)
                        else:
                            x = bh[r // 2, pl.ds(2 * LB * g + r % 2, LB, stride=2), :]
                        at = groups * r + g
                        here = lax.shift_right_logical(lane, 2) == at
                        lo = jnp.where(here, pltpu.roll(x, 4 * at, 1) if at else x, lo)
                        hi = jnp.where(here, pltpu.roll(x, (4 * at + 4) % LANES, 1), hi)
                pk[0, part] = lo
                pk[1, part] = hi

            @pl.when(up)
            def _():
                start_to(pk.at[0, 0], rxc.at[1, 1], h_send.at[2], h_recv.at[2], left, b - 1, w)
                start_to(pk.at[1, 0], rxc.at[1, 0], h_send.at[3], h_recv.at[3], right, b - 1, w)

            @pl.when(down)
            def _():
                start_to(pk.at[0, 0], rxc.at[0, 1], h_send.at[4], h_recv.at[4], left, b + 1, w)
                start_to(pk.at[1, 0], rxc.at[0, 0], h_send.at[5], h_recv.at[5], right, b + 1, w)

            start_to(pk.at[0], rx.at[1], h_send.at[0], h_recv.at[0], left, b, w)
            start_to(pk.at[1], rx.at[0], h_send.at[1], h_recv.at[1], right, b, w)
            for g in range(groups):
                part = pl.ds(2 * LB * g, 2 * LB)

                @pl.when(up)
                def _():
                    start_to(
                        b_up.at[part], r_far.at[1, part], h_send.at[6 + 2 * g], h_recv.at[6 + 2 * g], m, b - 1, w
                    )

                @pl.when(down)
                def _():
                    start_to(
                        b_down.at[part], r_far.at[0, part], h_send.at[7 + 2 * g], h_recv.at[7 + 2 * g], m, b + 1, w
                    )
        else:

            def gather(q, _):
                for i in range(2):
                    j = 2 * q + i
                    x = jnp.sum(et[:, j] * own, axis=0)
                    obuf[q, i] = (KEEP * DESCENT) * b1[member_rows(j), :] + DESCENT * x
                return 0

            lax.fori_loop(0, nm, gather, 0, unroll=2)
            top, bottom = edge_rows(gradient)
            top = (KEEP * DESCENT) * bh[0] + DESCENT * top
            bottom = (KEEP * DESCENT) * bh[1] + DESCENT * bottom
            for q in range(nm):
                obuf[q, 2, 0:4] = top[4 * q : 4 * q + 4]
                obuf[q, 2, 4:8] = bottom[4 * q : 4 * q + 4]

    c_in[:, :, mine] = obuf[m]

    def send_o(k, _):
        to = lax.rem(m + k, nm)
        start_to(obuf.at[to], c_in.at[:, :, mine], o_send, o_recv, to, b, w)
        return 0

    lax.fori_loop(1, nm, send_o, 0)
    drain(obuf.at[pl.ds(0, nm - 1)], o_recv)
    packed = c_in[2]
    for i in range(2):
        f = c_in[i]
        near = jnp.where(
            first,
            pltpu.roll(packed, LB - (2 * i + 1), 0),
            pltpu.roll(packed, 3 - 2 * i, 0),
        )
        far = jnp.where(
            first,
            pltpu.roll(packed, (LB - 2 * i) % LB, 0) if i else packed,
            pltpu.roll(packed, 2 - 2 * i, 0) if i == 0 else packed,
        )
        g = along(f, lon) + KAPPA * (
            jnp.where(first, near, pltpu.roll(f, 1, 0)) + jnp.where(last, near, pltpu.roll(f, LB - 1, 0))
        )
        e1 = (along(near, lon) + KAPPA * (far + f)) * edge
        h = along(g, lon) + KAPPA * (
            jnp.where(first, e1, pltpu.roll(g, 1, 0)) + jnp.where(last, e1, pltpu.roll(g, LB - 1, 0))
        )
        ctl_out[0, i] = (KEEP * KEEP) * cbuf[i] - h

    for i in range(vp):
        drain(et.at[0, pl.ds(0, members - 2)], e_send)
    for k in range(planes):
        drain(et.at[my_piece], k_send.at[k])
        drain(my_edges, k2_send.at[k])
        if k > 0:
            drain(et.at[my_piece], y_send.at[k])
            drain(my_edges, y2_send.at[k])
    drain(s_in.at[pl.ds(0, members - 2)], s_send.at[0])
    drain(obuf.at[pl.ds(0, nm - 1)], o_send)

    @pl.when(up)
    def _():
        drain(s_top, s_send.at[1])
        drain(dif.at[1], d_send.at[0])
        drain(e_up, g_send.at[0])
        drain(pk.at[0, 0], h_send.at[2])
        drain(pk.at[1, 0], h_send.at[3])
        for it in range(ITERS):
            drain(fstate.at[it, 1], f_send.at[4 * it])
            drain(bstate.at[it, 1], f_send.at[4 * it + 2])

    @pl.when(down)
    def _():
        drain(s_bot, s_send.at[2])
        drain(dif.at[1], d_send.at[1])
        drain(e_down, g_send.at[1])
        drain(pk.at[0, 0], h_send.at[4])
        drain(pk.at[1, 0], h_send.at[5])
        for it in range(ITERS):
            drain(fstate.at[it, 1], f_send.at[4 * it + 1])
            drain(bstate.at[it, 1], f_send.at[4 * it + 3])

    drain(pk.at[0], h_send.at[0])
    drain(pk.at[1], h_send.at[1])
    for g in range(groups):
        part = pl.ds(2 * LB * g, 2 * LB)

        @pl.when(up)
        def _():
            drain(b_up.at[part], h_send.at[6 + 2 * g])

        @pl.when(down)
        def _():
            drain(b_down.at[part], h_send.at[7 + 2 * g])

    for it in range(ITERS):

        @pl.when(before)
        def _():
            drain(fstate.at[it, 1], w_send.at[2 * it])

        @pl.when(after)
        def _():
            drain(ends_own.at[it], w_send.at[2 * it + 1])


def local_part(nm, nl, nw, *args):
    (
        ensemble,
        weights,
        diffusivity,
        coupling,
        tl_steps,
        obs_cell,
        obs_window,
        obs_value,
        obs_weight,
        error_weight,
    ) = args
    members = 2 * nm
    lon = nm * LANES
    planes = nw // 2
    groups = members // LB
    anywhere = pl.BlockSpec(memory_space=pltpu.HBM)
    obs = [x.reshape(-1, LANES) for x in (obs_cell, obs_window, obs_value, obs_weight)]
    tile = (LB, LANES)
    state = (NV, *tile)
    half = (4, LANES)

    def buf(*shape):
        return pltpu.VMEM(shape, F32)

    dma = pltpu.SemaphoreType.DMA
    return pl.pallas_call(
        functools.partial(kernel, nm, nl, nw),
        name="assimilate",
        out_shape=(
            pltpu.VMEM((1, 2, LB, lon), F32),
            pltpu.VMEM((1, *state), F32),
        ),
        in_specs=[anywhere] * 4 + [pl.BlockSpec(memory_space=pltpu.SMEM)] + [anywhere] * 5,
        out_specs=(pl.BlockSpec(memory_space=pltpu.VMEM),)*2,
        scratch_shapes=[
            pltpu.SMEM((NV, NV), F32),
            pltpu.SMEM((NV,), F32),
            pltpu.VMEM(obs[0].shape, jnp.int32),
            pltpu.VMEM(obs[0].shape, jnp.int32),
            buf(*obs[0].shape),
            buf(*obs[0].shape),
            buf(NV, members, *tile),
            buf(2, LB, lon),
            buf(2, LB, lon),
            buf(4, lon),
            buf(4, lon),
            buf(members, *tile),
            buf(nm, *half),
            buf(nm, *half),
            buf(3, *state),
            buf(ITERS, 3, *state),
            buf(ITERS, 3, *state),
            buf(ITERS, *state),
            buf(ITERS, 3, *state),
            buf(ITERS, 3, *state),
            buf(2 * NV * LB, LANES),
            buf(*state),
            buf(2 * members, LANES),
            buf(2 * members, LANES),
            buf(NV, 2, 2 * members, LANES),
            buf(members * LB, LANES),
            buf(2, 2 * members, LANES),
            buf(2 * members, LANES),
            buf(2 * members, LANES),
            buf(2, 2 * members, LANES),
            buf(2, 2, *tile),
            buf(2, 2, *tile),
            buf(2, 2, *tile),
            buf(members * LB, LANES),
            buf(nm, 3, *tile),
            buf(3, LB, lon),
            dma((12,)),
            dma,
            dma,
            dma((planes,)),
            dma((planes,)),
            dma((planes,)),
            dma((planes,)),
            dma((3,)),
            dma((3,)),
            dma((2,)),
            dma((2,)),
            dma((4 * ITERS,)),
            dma((4 * ITERS,)),
            dma((2 * ITERS,)),
            dma((2 * ITERS,)),
            dma((2,)),
            dma((2,)),
            dma((planes,)),
            dma((planes,)),
            dma((planes,)),
            dma((planes,)),
            dma((2 * groups + 6,)),
            dma((2 * groups + 6,)),
            dma,
            dma,
        ],
        compiler_params=pltpu.CompilerParams(
            collective_id=0, has_side_effects=True, vmem_limit_bytes=40 * 1024 * 1024
        ),
    )(
        *(pltpu.with_memory_space_constraint(x, pltpu.HBM) for x in (ensemble, weights, diffusivity, coupling)),
        tl_steps,
        *(pltpu.with_memory_space_constraint(x, pltpu.HBM) for x in (*obs, error_weight)),
    )


def solution(mesh):
    sizes = [mesh.shape[axis] for axis in ("mem", "lat", "win")]
    return jax.shard_map(
        functools.partial(local_part, *sizes),
        mesh=mesh,
        in_specs=(
            P("mem", None, "lat", None),
            P("win", "mem", "lat", None),
            P(None, "lat", "mem"),
            P(),
            P("win"),
            P(("mem", "lat")),
            P(("mem", "lat")),
            P(("mem", "lat")),
            P(("mem", "lat")),
            P(),
        ),
        out_specs=(P("win", "mem", "lat", None), P("win", None, "lat", "mem")),
        check_vma=False,
    )
```

```python
import functools
import math

import jax
import jax.numpy as jnp
from jax import lax
from jax.experimental import pallas as pl
from jax.experimental.pallas import tpu as pltpu
from jax.sharding import PartitionSpec as P

MESH = pl.DeviceIdType.MESH
NV = 8
LB = 8
LANES = 128
KMAX = 6
ITERS = 2
KAPPA = 0.125
DESCENT = 0.25
KEEP = 1.0 - DESCENT
CENTER = 1.0 - 4.0 * KAPPA
F32 = jnp.float32


def start_to(src, dst, send_sem, recv_sem, mem, lat, win):
    pltpu.make_async_remote_copy(
        src_ref=src,
        dst_ref=dst,
        send_sem=send_sem,
        recv_sem=recv_sem,
        device_id={"mem": mem, "lat": lat, "win": win},
        device_id_type=MESH,
    ).start()


def drain(ref, sem):
    pltpu.make_async_copy(ref, ref, sem).wait()


def along(f, lon):
    return CENTER * f + KAPPA * (pltpu.roll(f, 1, 1) + pltpu.roll(f, lon - 1, 1))


def kernel(
    nm,
    nl,
    nw,
    e_hbm,
    c_hbm,
    d_hbm,
    coup_hbm,
    steps,
    obs0,
    obs1,
    obs2,
    obs3,
    err_hbm,
    ctl_out,
    inc_out,
    coup,
    err_w,
    obs_cell,
    obs_window,
    obs_value,
    obs_weight,
    et,
    cbuf,
    sm,
    s_top,
    s_bot,
    s_in,
    r_top,
    r_bot,
    dif,
    fstate,
    bstate,
    inc_next,
    ends_own,
    ends_prev,
    wv,
    ewb,
    e_up,
    e_down,
    eh,
    b1,
    bh,
    b_up,
    b_down,
    r_far,
    pk,
    rx,
    rxc,
    sq,
    obuf,
    c_in,
    local,
    e_send,
    e_recv,
    y_send,
    y_recv,
    k_send,
    k_recv,
    s_send,
    s_recv,
    d_send,
    d_recv,
    f_send,
    f_recv,
    w_send,
    w_recv,
    g_send,
    g_recv,
    y2_send,
    y2_recv,
    k2_send,
    k2_recv,
    h_send,
    h_recv,
    o_send,
    o_recv,
):
    m, b, w = lax.axis_index("mem"), lax.axis_index("lat"), lax.axis_index("win")
    members = 2 * nm
    lon = nm * LANES
    vp = NV // nw
    scale = 1.0 / math.sqrt(members - 1)
    up, down = b > 0, b < nl - 1
    before, after = w > 0, w < nw - 1
    other = w + 1 - 2 * lax.rem(w, 2)
    planes = nw // 2
    groups = members // LB
    left, right = lax.rem(m + nm - 1, nm), lax.rem(m + 1, nm)
    mine = pl.ds(pl.multiple_of(m * LANES, LANES), LANES)
    my_pair = pl.ds(2 * m, 2)
    my_piece = pl.ds(w * vp, vp)

    load_c = pltpu.make_async_copy(c_hbm.at[0], cbuf, local.at[0])
    load_c.start()
    load_d = pltpu.make_async_copy(d_hbm, dif.at[1], local.at[1])
    load_d.start()
    small = [
        pltpu.make_async_copy(src, dst, local.at[5 + i])
        for i, (src, dst) in enumerate(
            (
                (coup_hbm, coup),
                (err_hbm, err_w),
                (obs0, obs_cell),
                (obs1, obs_window),
                (obs2, obs_value),
                (obs3, obs_weight),
            )
        )
    ]
    for copy in small:
        copy.start()
    for i in range(vp):
        pltpu.make_async_copy(
            e_hbm.at[:, w * vp + i, :, mine], et.at[w * vp + i, my_pair], local.at[2]
        ).start()

    barrier = pltpu.get_barrier_semaphore()

    def hello(mem, lat, win):
        pl.semaphore_signal(
            barrier, inc=1, device_id={"mem": mem, "lat": lat, "win": win}, device_id_type=MESH
        )

    def greet(k, _):
        hello(lax.rem(m + k, nm), b, w)
        return 0

    lax.fori_loop(1, nm, greet, 0)

    @pl.when(up)
    def _():
        hello(m, b - 1, w)

    @pl.when(down)
    def _():
        hello(m, b + 1, w)

    for k in range(1, planes):
        hello(m, b, lax.rem(w + 2 * k, nw))
    hello(m, b, other)
    odd = lax.rem(w, 2)

    @pl.when((odd == 0) & before)
    def _():
        hello(m, b, w - 1)

    @pl.when((odd == 1) & after)
    def _():
        hello(m, b, w + 1)

    one_more = jnp.where((w > 0) & (w < nw - 1), 1, 0)
    bands = jnp.where(up, 1, 0) + jnp.where(down, 1, 0)

    load_c.wait()
    row8 = lax.broadcasted_iota(jnp.int32, (LB, lon), 0)
    first, last = row8 == 0, row8 == LB - 1
    edge = jnp.where(first & up, 1.0, 0.0) + jnp.where(last & down, 1.0, 0.0)
    packed = jnp.where(row8 < 2, cbuf[0], cbuf[1])
    packed = jnp.where((row8 == 2) | (row8 == 3), pltpu.roll(cbuf[1], 2, 0), packed)
    packed = jnp.where((row8 == 4) | (row8 == 5), pltpu.roll(cbuf[0], LB - 2, 0), packed)
    s_top[...] = packed[0:4]
    s_bot[...] = packed[4:8]
    pl.semaphore_wait(barrier, nm - 1 + bands + planes + one_more)

    @pl.when(up)
    def _():
        start_to(s_top, r_bot, s_send.at[1], s_recv.at[1], m, b - 1, w)

    @pl.when(down)
    def _():
        start_to(s_bot, r_top, s_send.at[2], s_recv.at[2], m, b + 1, w)

    def send_e(k, _):
        to = lax.rem(m + k, nm)
        for i in range(vp):
            start_to(
                e_hbm.at[:, w * vp + i, :, pl.ds(pl.multiple_of(to * LANES, LANES), LANES)],
                et.at[w * vp + i, my_pair],
                e_send,
                e_recv,
                to,
                b,
                w,
            )
        return 0

    lax.fori_loop(1, nm, send_e, 0)

    @pl.when(jnp.logical_not(up))
    def _():
        dif[0] = jnp.zeros_like(dif[0])
        r_top[...] = jnp.zeros_like(r_top)
        r_far[0] = jnp.zeros_like(r_far[0])
        rxc[0] = jnp.zeros_like(rxc[0])
        for i in range(vp):
            eh[w * vp + i, 0] = jnp.zeros_like(r_far[0])
        for it in range(ITERS):
            fstate[it, 0] = jnp.zeros_like(fstate[it, 0])
            bstate[it, 0] = jnp.zeros_like(bstate[it, 0])

    @pl.when(jnp.logical_not(down))
    def _():
        dif[2] = jnp.zeros_like(dif[2])
        r_bot[...] = jnp.zeros_like(r_bot)
        r_far[1] = jnp.zeros_like(r_far[1])
        rxc[1] = jnp.zeros_like(rxc[1])
        for i in range(vp):
            eh[w * vp + i, 1] = jnp.zeros_like(r_far[1])
        for it in range(ITERS):
            fstate[it, 2] = jnp.zeros_like(fstate[it, 2])
            bstate[it, 2] = jnp.zeros_like(bstate[it, 2])

    @pl.when(jnp.logical_not(before))
    def _():
        ends_prev[...] = jnp.zeros_like(ends_prev)

    @pl.when(jnp.logical_not(after))
    def _():
        inc_next[...] = jnp.zeros_like(inc_next)

    for copy in small:
        copy.wait()
    for v in range(NV):
        ewb[v] = jnp.full((LB, LANES), err_w[v], F32)

    tall = lax.broadcasted_iota(jnp.int32, (NV * LB, LANES), 0)
    lane_of = lax.broadcasted_iota(jnp.int32, (LANES, LANES), 0)

    def add_obs(k, total):
        at = pl.ds(k, 1)
        cell = obs_cell[at, :]
        here = (tall == lax.shift_right_logical(cell, 7)) & (obs_window[at, :] == w)
        weight = jnp.where(here, obs_weight[at, :], 0.0)
        both = jnp.concatenate([weight, weight * obs_value[at, :]], axis=0)
        hot = jnp.where(lane_of == (cell & (LANES - 1)), 1.0, 0.0)
        return total + lax.dot_general(
            both,
            hot,
            (((1,), (1,)), ((), ())),
            precision=lax.Precision.HIGHEST,
            preferred_element_type=F32,
        )

    wv[...] = lax.fori_loop(
        0, obs_cell.shape[0], add_obs, jnp.zeros((2 * NV * LB, LANES), F32)
    )

    for i in range(vp):
        drain(et.at[w * vp + i, my_pair], local.at[2])
        drain(et.at[0, pl.ds(0, members - 2)], e_recv)
    start_to(et.at[my_piece], et.at[my_piece], k_send.at[0], k_recv.at[0], m, b, other)
    order = sorted(range(1, planes), key=lambda k: -min(k, planes - k))
    for k in order:
        start_to(
            et.at[my_piece], et.at[my_piece], y_send.at[k], y_recv.at[k], m, b, lax.rem(w + 2 * k, nw)
        )
    load_d.wait()

    @pl.when(up)
    def _():
        start_to(dif.at[1], dif.at[2], d_send.at[0], d_recv.at[0], m, b - 1, w)

    @pl.when(down)
    def _():
        start_to(dif.at[1], dif.at[0], d_send.at[1], d_recv.at[1], m, b + 1, w)

    def smooth_twice(f, packed, i):
        near = jnp.where(
            first,
            pltpu.roll(packed, LB - (2 * i + 1), 0),
            pltpu.roll(packed, 3 - 2 * i, 0),
        )
        far = jnp.where(
            first,
            pltpu.roll(packed, LB - 2, 0) if i else packed,
            packed if i else pltpu.roll(packed, 2, 0),
        )
        g = along(f, lon) + KAPPA * (
            jnp.where(first, near, pltpu.roll(f, 1, 0)) + jnp.where(last, near, pltpu.roll(f, LB - 1, 0))
        )
        e1 = (along(near, lon) + KAPPA * (far + f)) * edge
        return along(g, lon) + KAPPA * (
            jnp.where(first, e1, pltpu.roll(g, 1, 0)) + jnp.where(last, e1, pltpu.roll(g, LB - 1, 0))
        )

    @pl.when(up)
    def _():
        drain(r_top, s_recv.at[2])

    @pl.when(down)
    def _():
        drain(r_bot, s_recv.at[1])

    packed = jnp.concatenate([r_top[...], r_bot[...]], axis=0)
    for i in range(2):
        sm[i] = smooth_twice(cbuf[i], packed, i)

    def send_s(k, _):
        to = lax.rem(m + k, nm)
        cut = pl.ds(pl.multiple_of(to * LANES, LANES), LANES)
        start_to(sm.at[:, :, cut], s_in.at[my_pair], s_send.at[0], s_recv.at[0], to, b, w)
        return 0

    lax.fori_loop(1, nm, send_s, 0)
    s_in[my_pair] = sm[:, :, mine]
    drain(s_in.at[pl.ds(0, members - 2)], s_recv.at[0])

    def first_increment(v):
        fstate[0, 1, v] = jnp.sum(et[v] * s_in[...], axis=0) * scale

    for i in range(vp):
        v = w * vp + i
        for j in range(members):
            e_up[2 * j : 2 * j + 2, :] = et[v, j, 0:2]
            e_down[2 * j : 2 * j + 2, :] = et[v, j, 6:8]

        @pl.when(up)
        def _():
            start_to(e_up, eh.at[v, 1], g_send.at[0], g_recv.at[0], m, b - 1, w)

        @pl.when(down)
        def _():
            start_to(e_down, eh.at[v, 0], g_send.at[1], g_recv.at[1], m, b + 1, w)

        if i < vp - 1:

            @pl.when(up)
            def _():
                drain(e_up, g_send.at[0])

            @pl.when(down)
            def _():
                drain(e_down, g_send.at[1])

        first_increment(v)

    for k in reversed(order):
        origin = lax.rem(w - 2 * k + nw, nw) * vp
        piece = et.at[pl.ds(origin, vp)]
        drain(piece, y_recv.at[k])
        start_to(piece, piece, k_send.at[k], k_recv.at[k], m, b, other)
        for i in range(vp):
            first_increment(origin + i)
    for k in [0, *reversed(order)]:
        origin = lax.rem(other - 2 * k + nw, nw) * vp
        drain(et.at[pl.ds(origin, vp)], k_recv.at[k])
        for i in range(vp):
            first_increment(origin + i)

    rows24 = lax.broadcasted_iota(jnp.int32, (3 * LB, LANES), 0)
    inside24 = ((rows24 >= LB) | up) & ((rows24 < 2 * LB) | down)
    lane = lax.broadcasted_iota(jnp.int32, (LB, LANES), 1)
    row = lax.broadcasted_iota(jnp.int32, (LB, LANES), 0)
    up_f = jnp.where(up, 1.0, 0.0)
    down_f = jnp.where(down, 1.0, 0.0)

    def wide(ref):
        return jnp.concatenate([ref[0], ref[1], ref[2]], axis=1)

    def second(x):
        return pltpu.roll(x, 1, 1) + pltpu.roll(x, 3 * LB - 1, 1) - 2.0 * x

    def mixed(x, transposed):
        rows = []
        for v in range(NV):
            total = None
            for u in range(NV):
                term = (coup[u, v] if transposed else coup[v, u]) * x[u]
                total = term if total is None else total + term
            rows.append(total)
        return jnp.stack(rows, axis=0)

    count = jnp.full((3 * LB, LANES), steps[0], jnp.int32)

    def halo(ref, it, which):
        base = 4 * it + 2 * which

        @pl.when(up)
        def _():
            start_to(ref.at[it, 1], ref.at[it, 2], f_send.at[base], f_recv.at[base], m, b - 1, w)

        @pl.when(down)
        def _():
            start_to(ref.at[it, 1], ref.at[it, 0], f_send.at[base + 1], f_recv.at[base + 1], m, b + 1, w)

    def halo_wait(ref, it, which):
        base = 4 * it + 2 * which

        @pl.when(down)
        def _():
            drain(ref.at[it, 2], f_recv.at[base])

        @pl.when(up)
        def _():
            drain(ref.at[it, 0], f_recv.at[base + 1])

    my_edges = eh.at[my_piece]

    def send_edges():
        for i in range(vp):

            @pl.when(down)
            def _():
                drain(eh.at[0, 1], g_recv.at[0])

            @pl.when(up)
            def _():
                drain(eh.at[0, 0], g_recv.at[1])

        start_to(my_edges, my_edges, k2_send.at[0], k2_recv.at[0], m, b, other)
        for k in order:
            start_to(my_edges, my_edges, y2_send.at[k], y2_recv.at[k], m, b, lax.rem(w + 2 * k, nw))

    def pass_edges():
        for k in reversed(order):
            piece = eh.at[pl.ds(lax.rem(w - 2 * k + nw, nw) * vp, vp)]
            drain(piece, y2_recv.at[k])
            start_to(piece, piece, k2_send.at[k], k2_recv.at[k], m, b, other)

    def rows_of(ref, first_row, stride, g):
        return ref[pl.ds(g * LB * stride + first_row, LB, stride=stride), :]

    def beside(x, y, to_left):
        shift, end = (1, lane == 0) if to_left else (LANES - 1, lane == LANES - 1)
        return jnp.where(end, pltpu.roll(y, shift, 2), pltpu.roll(x, shift, 2))

    def masked(x, depth):
        n = x.shape[0]
        return jnp.concatenate([x[:depth] * up_f, x[depth : n - depth], x[n - depth :] * down_f], axis=0)

    def smooth_group(g):
        main = [r_far[0, pl.ds(2 * LB * g + r, LB, stride=2), :] for r in range(2)]
        main += [bh[0, pl.ds(2 * LB * g + r, LB, stride=2), :] for r in range(2)]
        main += [rows_of(b1, r, LB, g) for r in range(LB)]
        main += [bh[1, pl.ds(2 * LB * g + r, LB, stride=2), :] for r in range(2)]
        main += [r_far[1, pl.ds(2 * LB * g + r, LB, stride=2), :] for r in range(2)]
        places = [(rxc, 0, 4), (rxc, 0, 5), (rx, 1, 0), (rx, 1, 1)]
        places += [(rx, 0, r) for r in range(LB)]
        places += [(rx, 1, 2), (rx, 1, 3), (rxc, 1, 2), (rxc, 1, 3)]
        sides = []
        for ref, which, r in places:
            at = 4 * (groups * r + g)
            lo, hi = (ref[which, 0], ref[which, 1]) if ref is rxc else (ref[0, which], ref[1, which])
            from_left = pltpu.roll(lo, LANES - 4 - at, 1)
            from_right = pltpu.roll(hi, (LANES - at) % LANES, 1)
            sides.append(jnp.where(lane < 4, from_right, jnp.where(lane >= LANES - 4, from_left, 0.0)))
        f0, f1 = jnp.stack(main, axis=0), jnp.stack(sides, axis=0)
        for depth in (3, 2, 1, 0):
            m0, m1 = f0[1:-1], f1[1:-1]
            n0 = beside(m0, m1, True) + beside(m0, m1, False) + f0[2:] + f0[:-2]
            n1 = beside(m1, m0, True) + beside(m1, m0, False) + f1[2:] + f1[:-2]
            f0 = CENTER * m0 + KAPPA * n0
            f1 = CENTER * m1 + KAPPA * n1
            if depth:
                f0, f1 = masked(f0, depth), masked(f1, depth)
        for r in range(LB):
            sq[pl.ds(LB * LB * g + r, LB, stride=LB), :] = f0[r]

    def member_rows(j):
        return pl.ds(pl.multiple_of(LB * j, LB), LB)

    def fourfold(x, from_row):
        x = jnp.where((row == from_row) | (row == from_row + 1), x, 0.0)
        x = x + pltpu.roll(x, 2, 1)
        return x + pltpu.roll(x, 4, 1)

    def edge_rows(gradient):
        out = []
        for side, part in enumerate((gradient[:, :LB], gradient[:, 2 * LB :])):
            tile = fourfold(part, 0 if side else LB - 2)
            rows = eh[:, side].reshape(NV, groups * 2, LB, LANES)
            out.append(jnp.sum(rows * tile[:, None], axis=0).reshape(2 * members, LANES))
        return out

    for it in range(ITERS):
        if it > 0:
            total = jnp.zeros((NV, LB, LANES), F32)
            drain(rx.at[1], h_recv.at[0])
            drain(rx.at[0], h_recv.at[1])

            @pl.when(down)
            def _():
                drain(rxc.at[1, 1], h_recv.at[2])
                drain(rxc.at[1, 0], h_recv.at[3])

            @pl.when(up)
            def _():
                drain(rxc.at[0, 1], h_recv.at[4])
                drain(rxc.at[0, 0], h_recv.at[5])

            def add_member(j, total):
                return total + et[:, j] * sq[member_rows(j), :][None]

            for g in range(groups):
                part = pl.ds(2 * LB * g, 2 * LB)

                @pl.when(down)
                def _():
                    drain(r_far.at[1, part], h_recv.at[6 + 2 * g])

                @pl.when(up)
                def _():
                    drain(r_far.at[0, part], h_recv.at[7 + 2 * g])

                smooth_group(g)
                total = lax.fori_loop(LB * g, LB * (g + 1), add_member, total, unroll=True)
            fstate[it, 1] = KEEP * fstate[it - 1, 1] - (DESCENT * scale) * total

        halo(fstate, it, 0)

        @pl.when(before)
        def _():
            start_to(
                fstate.at[it, 1], inc_next.at[it], w_send.at[2 * it], w_recv.at[2 * it], m, b, w - 1
            )

        if it == ITERS - 1:
            inc_out[0] = fstate[it, 1]
        else:
            send_edges()

            @pl.when(up)
            def _():
                drain(dif.at[0], d_recv.at[1])

            @pl.when(down)
            def _():
                drain(dif.at[2], d_recv.at[0])

        halo_wait(fstate, it, 0)
        coeff = wide(dif)

        def forth(k, u):
            moved = u + coeff * second(u) + mixed(u, False)
            moved = jnp.where(inside24, moved, 0.0)
            return jnp.where(k < count, moved, u)

        state = lax.fori_loop(0, KMAX, forth, wide(fstate.at[it]))
        ends = state[:, LB : 2 * LB]
        for part in range(3):
            ends_own[it, part] = state[:, LB * part : LB * (part + 1)]

        @pl.when(after)
        def _():
            start_to(
                ends_own.at[it],
                ends_prev.at[it],
                w_send.at[2 * it + 1],
                w_recv.at[2 * it + 1],
                m,
                b,
                w + 1,
            )

        @pl.when(after)
        def _():
            drain(inc_next.at[it], w_recv.at[2 * it])

        dense = wv[...].reshape(2, NV, LB, LANES)
        to_next = jnp.where(after, ewb[...] * (ends - inc_next[it]), 0.0)
        bstate[it, 1] = dense[0] * ends - dense[1] + to_next
        halo(bstate, it, 1)
        if it == 0:
            pass_edges()
        halo_wait(bstate, it, 1)

        def back(k, y):
            moved = y + second(coeff * y) + mixed(y, True)
            moved = jnp.where(inside24, moved, 0.0)
            return jnp.where(KMAX - 1 - k < count, moved, y)

        state = lax.fori_loop(0, KMAX, back, wide(bstate.at[it]))

        @pl.when(before)
        def _():
            drain(ends_prev.at[it], w_recv.at[2 * it + 1])

        wide_w = jnp.concatenate([ewb[...]] * 3, axis=1)
        misfit = jnp.where(before, wide_w * (wide(ends_prev.at[it]) - wide(fstate.at[it])), 0.0)
        gradient = (state - misfit) * scale
        own = gradient[:, LB : 2 * LB]

        if it == 0:

            def spread(j, _):
                b1[member_rows(j), :] = jnp.sum(et[:, j] * own, axis=0)
                return 0

            lax.fori_loop(0, members, spread, 0, unroll=4)
            for g in range(groups):
                for r in range(2):
                    to_row = pl.ds(2 * LB * g + r, LB, stride=2)
                    b_up[to_row, :] = rows_of(b1, 2 + r, LB, g)
                    b_down[to_row, :] = rows_of(b1, 4 + r, LB, g)

            for k in range(planes):
                drain(my_edges, k2_recv.at[k])
            top, bottom = edge_rows(gradient)
            bh[0] = top
            bh[1] = bottom
            for part in range(2):
                lo = hi = jnp.zeros((LB, LANES), F32)
                for r in range(LB if part == 0 else 4):
                    for g in range(groups):
                        if part == 0:
                            x = rows_of(b1, r, LB, g)
                        else:
                            x = bh[r // 2, pl.ds(2 * LB * g + r % 2, LB, stride=2), :]
                        at = groups * r + g
                        here = lax.shift_right_logical(lane, 2) == at
                        lo = jnp.where(here, pltpu.roll(x, 4 * at, 1) if at else x, lo)
                        hi = jnp.where(here, pltpu.roll(x, (4 * at + 4) % LANES, 1), hi)
                pk[0, part] = lo
                pk[1, part] = hi

            @pl.when(up)
            def _():
                start_to(pk.at[0, 0], rxc.at[1, 1], h_send.at[2], h_recv.at[2], left, b - 1, w)
                start_to(pk.at[1, 0], rxc.at[1, 0], h_send.at[3], h_recv.at[3], right, b - 1, w)

            @pl.when(down)
            def _():
                start_to(pk.at[0, 0], rxc.at[0, 1], h_send.at[4], h_recv.at[4], left, b + 1, w)
                start_to(pk.at[1, 0], rxc.at[0, 0], h_send.at[5], h_recv.at[5], right, b + 1, w)

            start_to(pk.at[0], rx.at[1], h_send.at[0], h_recv.at[0], left, b, w)
            start_to(pk.at[1], rx.at[0], h_send.at[1], h_recv.at[1], right, b, w)
            for g in range(groups):
                part = pl.ds(2 * LB * g, 2 * LB)

                @pl.when(up)
                def _():
                    start_to(
                        b_up.at[part], r_far.at[1, part], h_send.at[6 + 2 * g], h_recv.at[6 + 2 * g], m, b - 1, w
                    )

                @pl.when(down)
                def _():
                    start_to(
                        b_down.at[part], r_far.at[0, part], h_send.at[7 + 2 * g], h_recv.at[7 + 2 * g], m, b + 1, w
                    )
        else:

            def gather(q, _):
                for i in range(2):
                    j = 2 * q + i
                    x = jnp.sum(et[:, j] * own, axis=0)
                    obuf[q, i] = (KEEP * DESCENT) * b1[member_rows(j), :] + DESCENT * x
                return 0

            lax.fori_loop(0, nm, gather, 0, unroll=2)
            top, bottom = edge_rows(gradient)
            top = (KEEP * DESCENT) * bh[0] + DESCENT * top
            bottom = (KEEP * DESCENT) * bh[1] + DESCENT * bottom
            for q in range(nm):
                obuf[q, 2, 0:4] = top[4 * q : 4 * q + 4]
                obuf[q, 2, 4:8] = bottom[4 * q : 4 * q + 4]

    c_in[:, :, mine] = obuf[m]

    def send_o(k, _):
        to = lax.rem(m + k, nm)
        start_to(obuf.at[to], c_in.at[:, :, mine], o_send, o_recv, to, b, w)
        return 0

    lax.fori_loop(1, nm, send_o, 0)
    drain(obuf.at[pl.ds(0, nm - 1)], o_recv)
    packed = c_in[2]
    for i in range(2):
        h = smooth_twice(c_in[i], packed, i)
        ctl_out[0, i] = (KEEP * KEEP) * cbuf[i] - h

    for i in range(vp):
        drain(et.at[0, pl.ds(0, members - 2)], e_send)
    for k in range(planes):
        drain(et.at[my_piece], k_send.at[k])
        drain(my_edges, k2_send.at[k])
        if k > 0:
            drain(et.at[my_piece], y_send.at[k])
            drain(my_edges, y2_send.at[k])
    drain(s_in.at[pl.ds(0, members - 2)], s_send.at[0])
    drain(obuf.at[pl.ds(0, nm - 1)], o_send)

    @pl.when(up)
    def _():
        drain(s_top, s_send.at[1])
        drain(dif.at[1], d_send.at[0])
        drain(e_up, g_send.at[0])
        drain(pk.at[0, 0], h_send.at[2])
        drain(pk.at[1, 0], h_send.at[3])
        for it in range(ITERS):
            drain(fstate.at[it, 1], f_send.at[4 * it])
            drain(bstate.at[it, 1], f_send.at[4 * it + 2])

    @pl.when(down)
    def _():
        drain(s_bot, s_send.at[2])
        drain(dif.at[1], d_send.at[1])
        drain(e_down, g_send.at[1])
        drain(pk.at[0, 0], h_send.at[4])
        drain(pk.at[1, 0], h_send.at[5])
        for it in range(ITERS):
            drain(fstate.at[it, 1], f_send.at[4 * it + 1])
            drain(bstate.at[it, 1], f_send.at[4 * it + 3])

    drain(pk.at[0], h_send.at[0])
    drain(pk.at[1], h_send.at[1])
    for g in range(groups):
        part = pl.ds(2 * LB * g, 2 * LB)

        @pl.when(up)
        def _():
            drain(b_up.at[part], h_send.at[6 + 2 * g])

        @pl.when(down)
        def _():
            drain(b_down.at[part], h_send.at[7 + 2 * g])

    for it in range(ITERS):

        @pl.when(before)
        def _():
            drain(fstate.at[it, 1], w_send.at[2 * it])

        @pl.when(after)
        def _():
            drain(ends_own.at[it], w_send.at[2 * it + 1])


def local_part(nm, nl, nw, *args):
    (
        ensemble,
        weights,
        diffusivity,
        coupling,
        tl_steps,
        obs_cell,
        obs_window,
        obs_value,
        obs_weight,
        error_weight,
    ) = args
    members = 2 * nm
    lon = nm * LANES
    planes = nw // 2
    groups = members // LB
    anywhere = pl.BlockSpec(memory_space=pltpu.HBM)
    obs = [x.reshape(-1, LANES) for x in (obs_cell, obs_window, obs_value, obs_weight)]
    tile = (LB, LANES)
    state = (NV, *tile)

    def buf(*shape):
        return pltpu.VMEM(shape, F32)

    dma = pltpu.SemaphoreType.DMA
    return pl.pallas_call(
        functools.partial(kernel, nm, nl, nw),
        name="assimilate",
        out_shape=(
            pltpu.VMEM((1, 2, LB, lon), F32),
            pltpu.VMEM((1, *state), F32),
        ),
        in_specs=[anywhere] * 4 + [pl.BlockSpec(memory_space=pltpu.SMEM)] + [anywhere] * 5,
        out_specs=(pl.BlockSpec(memory_space=pltpu.VMEM),)*2,
        scratch_shapes=[
            pltpu.SMEM((NV, NV), F32),
            pltpu.SMEM((NV,), F32),
            pltpu.VMEM(obs[0].shape, jnp.int32),
            pltpu.VMEM(obs[0].shape, jnp.int32),
            buf(*obs[0].shape),
            buf(*obs[0].shape),
            buf(NV, members, *tile),
            buf(2, LB, lon),
            buf(2, LB, lon),
            buf(4, lon),
            buf(4, lon),
            buf(members, *tile),
            buf(4, lon),
            buf(4, lon),
            buf(3, *state),
            buf(ITERS, 3, *state),
            buf(ITERS, 3, *state),
            buf(ITERS, *state),
            buf(ITERS, 3, *state),
            buf(ITERS, 3, *state),
            buf(2 * NV * LB, LANES),
            buf(*state),
            buf(2 * members, LANES),
            buf(2 * members, LANES),
            buf(NV, 2, 2 * members, LANES),
            buf(members * LB, LANES),
            buf(2, 2 * members, LANES),
            buf(2 * members, LANES),
            buf(2 * members, LANES),
            buf(2, 2 * members, LANES),
            buf(2, 2, *tile),
            buf(2, 2, *tile),
            buf(2, 2, *tile),
            buf(members * LB, LANES),
            buf(nm, 3, *tile),
            buf(3, LB, lon),
            dma((12,)),
            dma,
            dma,
            dma((planes,)),
            dma((planes,)),
            dma((planes,)),
            dma((planes,)),
            dma((3,)),
            dma((3,)),
            dma((2,)),
            dma((2,)),
            dma((4 * ITERS,)),
            dma((4 * ITERS,)),
            dma((2 * ITERS,)),
            dma((2 * ITERS,)),
            dma((2,)),
            dma((2,)),
            dma((planes,)),
            dma((planes,)),
            dma((planes,)),
            dma((planes,)),
            dma((2 * groups + 6,)),
            dma((2 * groups + 6,)),
            dma,
            dma,
        ],
        compiler_params=pltpu.CompilerParams(
            collective_id=0, has_side_effects=True, vmem_limit_bytes=40 * 1024 * 1024
        ),
    )(
        *(pltpu.with_memory_space_constraint(x, pltpu.HBM) for x in (ensemble, weights, diffusivity, coupling)),
        tl_steps,
        *(pltpu.with_memory_space_constraint(x, pltpu.HBM) for x in (*obs, error_weight)),
    )


def solution(mesh):
    sizes = [mesh.shape[axis] for axis in ("mem", "lat", "win")]
    return jax.shard_map(
        functools.partial(local_part, *sizes),
        mesh=mesh,
        in_specs=(
            P("mem", None, "lat", None),
            P("win", "mem", "lat", None),
            P(None, "lat", "mem"),
            P(),
            P("win"),
            P(("mem", "lat")),
            P(("mem", "lat")),
            P(("mem", "lat")),
            P(("mem", "lat")),
            P(),
        ),
        out_specs=(P("win", "mem", "lat", None), P("win", None, "lat", "mem")),
        check_vma=False,
    )
```

```python
import functools
import math

import jax
import jax.numpy as jnp
from jax import lax
from jax.experimental import pallas as pl
from jax.experimental.pallas import tpu as pltpu
from jax.sharding import PartitionSpec as P

MESH = pl.DeviceIdType.MESH
NV = 8
LB = 8
LANES = 128
KMAX = 6
ITERS = 2
KAPPA = 0.125
DESCENT = 0.25
KEEP = 1.0 - DESCENT
CENTER = 1.0 - 4.0 * KAPPA
F32 = jnp.float32


def start_to(src, dst, send_sem, recv_sem, mem, lat, win):
    pltpu.make_async_remote_copy(
        src_ref=src,
        dst_ref=dst,
        send_sem=send_sem,
        recv_sem=recv_sem,
        device_id={"mem": mem, "lat": lat, "win": win},
        device_id_type=MESH,
    ).start()


def drain(ref, sem):
    pltpu.make_async_copy(ref, ref, sem).wait()


def along(f, lon):
    return CENTER * f + KAPPA * (pltpu.roll(f, 1, 1) + pltpu.roll(f, lon - 1, 1))


def kernel(
    nm,
    nl,
    nw,
    e_hbm,
    c_hbm,
    d_hbm,
    coup_hbm,
    steps,
    obs0,
    obs1,
    obs2,
    obs3,
    err_hbm,
    ctl_out,
    inc_out,
    coup,
    err_w,
    obs_cell,
    obs_window,
    obs_value,
    obs_weight,
    et,
    cbuf,
    sm,
    s_top,
    s_bot,
    s_in,
    r_top,
    r_bot,
    dif,
    fstate,
    bstate,
    inc_next,
    ends_own,
    ends_prev,
    wv,
    ewb,
    e_up,
    e_down,
    eh,
    b1,
    bh,
    b_up,
    b_down,
    r_far,
    pk,
    rx,
    rxc,
    sq,
    obuf,
    c_in,
    local,
    e_send,
    e_recv,
    y_send,
    y_recv,
    k_send,
    k_recv,
    s_send,
    s_recv,
    d_send,
    d_recv,
    f_send,
    f_recv,
    w_send,
    w_recv,
    g_send,
    g_recv,
    y2_send,
    y2_recv,
    k2_send,
    k2_recv,
    h_send,
    h_recv,
    o_send,
    o_recv,
):
    m, b, w = lax.axis_index("mem"), lax.axis_index("lat"), lax.axis_index("win")
    members = 2 * nm
    lon = nm * LANES
    vp = NV // nw
    scale = 1.0 / math.sqrt(members - 1)
    up, down = b > 0, b < nl - 1
    before, after = w > 0, w < nw - 1
    other = w + 1 - 2 * lax.rem(w, 2)
    planes = nw // 2
    groups = members // LB
    left, right = lax.rem(m + nm - 1, nm), lax.rem(m + 1, nm)
    mine = pl.ds(pl.multiple_of(m * LANES, LANES), LANES)
    my_pair = pl.ds(2 * m, 2)
    my_piece = pl.ds(w * vp, vp)

    load_c = pltpu.make_async_copy(c_hbm.at[0], cbuf, local.at[0])
    load_c.start()
    load_d = pltpu.make_async_copy(d_hbm, dif.at[1], local.at[1])
    load_d.start()
    small = [
        pltpu.make_async_copy(src, dst, local.at[5 + i])
        for i, (src, dst) in enumerate(
            (
                (coup_hbm, coup),
                (err_hbm, err_w),
                (obs0, obs_cell),
                (obs1, obs_window),
                (obs2, obs_value),
                (obs3, obs_weight),
            )
        )
    ]
    for copy in small:
        copy.start()
    for i in range(vp):
        pltpu.make_async_copy(
            e_hbm.at[:, w * vp + i, :, mine], et.at[w * vp + i, my_pair], local.at[2]
        ).start()

    barrier = pltpu.get_barrier_semaphore()

    def hello(mem, lat, win):
        pl.semaphore_signal(
            barrier, inc=1, device_id={"mem": mem, "lat": lat, "win": win}, device_id_type=MESH
        )

    def greet(k, _):
        hello(lax.rem(m + k, nm), b, w)
        return 0

    lax.fori_loop(1, nm, greet, 0)

    @pl.when(up)
    def _():
        hello(m, b - 1, w)

    @pl.when(down)
    def _():
        hello(m, b + 1, w)

    for k in range(1, planes):
        hello(m, b, lax.rem(w + 2 * k, nw))
    hello(m, b, other)
    odd = lax.rem(w, 2)

    @pl.when((odd == 0) & before)
    def _():
        hello(m, b, w - 1)

    @pl.when((odd == 1) & after)
    def _():
        hello(m, b, w + 1)

    one_more = jnp.where((w > 0) & (w < nw - 1), 1, 0)
    bands = jnp.where(up, 1, 0) + jnp.where(down, 1, 0)

    load_c.wait()
    row8 = lax.broadcasted_iota(jnp.int32, (LB, lon), 0)
    first, last = row8 == 0, row8 == LB - 1
    edge = jnp.where(first & up, 1.0, 0.0) + jnp.where(last & down, 1.0, 0.0)
    packed = jnp.where(row8 < 2, cbuf[0], cbuf[1])
    packed = jnp.where((row8 == 2) | (row8 == 3), pltpu.roll(cbuf[1], 2, 0), packed)
    packed = jnp.where((row8 == 4) | (row8 == 5), pltpu.roll(cbuf[0], LB - 2, 0), packed)
    s_top[...] = packed[0:4]
    s_bot[...] = packed[4:8]
    pl.semaphore_wait(barrier, nm - 1 + bands + planes + one_more)

    @pl.when(up)
    def _():
        start_to(s_top, r_bot, s_send.at[1], s_recv.at[1], m, b - 1, w)

    @pl.when(down)
    def _():
        start_to(s_bot, r_top, s_send.at[2], s_recv.at[2], m, b + 1, w)

    def send_e(k, _):
        to = lax.rem(m + k, nm)
        for i in range(vp):
            start_to(
                e_hbm.at[:, w * vp + i, :, pl.ds(pl.multiple_of(to * LANES, LANES), LANES)],
                et.at[w * vp + i, my_pair],
                e_send,
                e_recv,
                to,
                b,
                w,
            )
        return 0

    lax.fori_loop(1, nm, send_e, 0)

    @pl.when(jnp.logical_not(up))
    def _():
        dif[0] = jnp.zeros_like(dif[0])
        r_top[...] = jnp.zeros_like(r_top)
        r_far[0] = jnp.zeros_like(r_far[0])
        rxc[0] = jnp.zeros_like(rxc[0])
        for i in range(vp):
            eh[w * vp + i, 0] = jnp.zeros_like(r_far[0])
        for it in range(ITERS):
            fstate[it, 0] = jnp.zeros_like(fstate[it, 0])
            bstate[it, 0] = jnp.zeros_like(bstate[it, 0])

    @pl.when(jnp.logical_not(down))
    def _():
        dif[2] = jnp.zeros_like(dif[2])
        r_bot[...] = jnp.zeros_like(r_bot)
        r_far[1] = jnp.zeros_like(r_far[1])
        rxc[1] = jnp.zeros_like(rxc[1])
        for i in range(vp):
            eh[w * vp + i, 1] = jnp.zeros_like(r_far[1])
        for it in range(ITERS):
            fstate[it, 2] = jnp.zeros_like(fstate[it, 2])
            bstate[it, 2] = jnp.zeros_like(bstate[it, 2])

    @pl.when(jnp.logical_not(before))
    def _():
        ends_prev[...] = jnp.zeros_like(ends_prev)

    @pl.when(jnp.logical_not(after))
    def _():
        inc_next[...] = jnp.zeros_like(inc_next)

    for copy in small:
        copy.wait()
    for v in range(NV):
        ewb[v] = jnp.full((LB, LANES), err_w[v], F32)

    tall = lax.broadcasted_iota(jnp.int32, (NV * LB, LANES), 0)
    lane_of = lax.broadcasted_iota(jnp.int32, (LANES, LANES), 0)

    def add_obs(k, total):
        at = pl.ds(k, 1)
        cell = obs_cell[at, :]
        here = (tall == lax.shift_right_logical(cell, 7)) & (obs_window[at, :] == w)
        weight = jnp.where(here, obs_weight[at, :], 0.0)
        both = jnp.concatenate([weight, weight * obs_value[at, :]], axis=0)
        hot = jnp.where(lane_of == (cell & (LANES - 1)), 1.0, 0.0)
        return total + lax.dot_general(
            both,
            hot,
            (((1,), (1,)), ((), ())),
            precision=lax.Precision.HIGHEST,
            preferred_element_type=F32,
        )

    wv[...] = lax.fori_loop(
        0, obs_cell.shape[0], add_obs, jnp.zeros((2 * NV * LB, LANES), F32)
    )

    def smooth_twice(f, packed, i):
        near = jnp.where(
            first,
            pltpu.roll(packed, LB - (2 * i + 1), 0),
            pltpu.roll(packed, 3 - 2 * i, 0),
        )
        far = jnp.where(
            first,
            pltpu.roll(packed, LB - 2, 0) if i else packed,
            packed if i else pltpu.roll(packed, 2, 0),
        )
        g = along(f, lon) + KAPPA * (
            jnp.where(first, near, pltpu.roll(f, 1, 0)) + jnp.where(last, near, pltpu.roll(f, LB - 1, 0))
        )
        e1 = (along(near, lon) + KAPPA * (far + f)) * edge
        return along(g, lon) + KAPPA * (
            jnp.where(first, e1, pltpu.roll(g, 1, 0)) + jnp.where(last, e1, pltpu.roll(g, LB - 1, 0))
        )

    @pl.when(up)
    def _():
        drain(r_top, s_recv.at[2])

    @pl.when(down)
    def _():
        drain(r_bot, s_recv.at[1])

    packed = jnp.concatenate([r_top[...], r_bot[...]], axis=0)
    for i in range(2):
        sm[i] = smooth_twice(cbuf[i], packed, i)

    def send_s(k, _):
        to = lax.rem(m + k, nm)
        cut = pl.ds(pl.multiple_of(to * LANES, LANES), LANES)
        start_to(sm.at[:, :, cut], s_in.at[my_pair], s_send.at[0], s_recv.at[0], to, b, w)
        return 0

    lax.fori_loop(1, nm, send_s, 0)
    for i in range(vp):
        drain(et.at[w * vp + i, my_pair], local.at[2])
        drain(et.at[0, pl.ds(0, members - 2)], e_recv)
    start_to(et.at[my_piece], et.at[my_piece], k_send.at[0], k_recv.at[0], m, b, other)
    order = sorted(range(1, planes), key=lambda k: -min(k, planes - k))
    for k in order:
        start_to(
            et.at[my_piece], et.at[my_piece], y_send.at[k], y_recv.at[k], m, b, lax.rem(w + 2 * k, nw)
        )
    s_in[my_pair] = sm[:, :, mine]
    drain(s_in.at[pl.ds(0, members - 2)], s_recv.at[0])
    load_d.wait()

    @pl.when(up)
    def _():
        start_to(dif.at[1], dif.at[2], d_send.at[0], d_recv.at[0], m, b - 1, w)

    @pl.when(down)
    def _():
        start_to(dif.at[1], dif.at[0], d_send.at[1], d_recv.at[1], m, b + 1, w)


    def first_increment(v):
        fstate[0, 1, v] = jnp.sum(et[v] * s_in[...], axis=0) * scale

        @pl.when(up)
        def _():
            start_to(fstate.at[0, 1, v], fstate.at[0, 2, v], f_send.at[0], f_recv.at[0], m, b - 1, w)

        @pl.when(down)
        def _():
            start_to(fstate.at[0, 1, v], fstate.at[0, 0, v], f_send.at[1], f_recv.at[1], m, b + 1, w)

    for i in range(vp):
        v = w * vp + i
        for j in range(members):
            e_up[2 * j : 2 * j + 2, :] = et[v, j, 0:2]
            e_down[2 * j : 2 * j + 2, :] = et[v, j, 6:8]

        @pl.when(up)
        def _():
            start_to(e_up, eh.at[v, 1], g_send.at[0], g_recv.at[0], m, b - 1, w)

        @pl.when(down)
        def _():
            start_to(e_down, eh.at[v, 0], g_send.at[1], g_recv.at[1], m, b + 1, w)

        if i < vp - 1:

            @pl.when(up)
            def _():
                drain(e_up, g_send.at[0])

            @pl.when(down)
            def _():
                drain(e_down, g_send.at[1])

        first_increment(v)

    for k in reversed(order):
        origin = lax.rem(w - 2 * k + nw, nw) * vp
        piece = et.at[pl.ds(origin, vp)]
        drain(piece, y_recv.at[k])
        start_to(piece, piece, k_send.at[k], k_recv.at[k], m, b, other)
        for i in range(vp):
            first_increment(origin + i)
    for k in [0, *reversed(order)]:
        origin = lax.rem(other - 2 * k + nw, nw) * vp
        drain(et.at[pl.ds(origin, vp)], k_recv.at[k])
        for i in range(vp):
            first_increment(origin + i)

    rows24 = lax.broadcasted_iota(jnp.int32, (3 * LB, LANES), 0)
    inside24 = ((rows24 >= LB) | up) & ((rows24 < 2 * LB) | down)
    lane = lax.broadcasted_iota(jnp.int32, (LB, LANES), 1)
    row = lax.broadcasted_iota(jnp.int32, (LB, LANES), 0)
    up_f = jnp.where(up, 1.0, 0.0)
    down_f = jnp.where(down, 1.0, 0.0)

    def wide(ref):
        return jnp.concatenate([ref[0], ref[1], ref[2]], axis=1)

    def second(x):
        return pltpu.roll(x, 1, 1) + pltpu.roll(x, 3 * LB - 1, 1) - 2.0 * x

    def mixed(x, transposed):
        rows = []
        for v in range(NV):
            total = None
            for u in range(NV):
                term = (coup[u, v] if transposed else coup[v, u]) * x[u]
                total = term if total is None else total + term
            rows.append(total)
        return jnp.stack(rows, axis=0)

    count = jnp.full((3 * LB, LANES), steps[0], jnp.int32)

    def halo(ref, it, which):
        base = 4 * it + 2 * which

        @pl.when(up)
        def _():
            start_to(ref.at[it, 1], ref.at[it, 2], f_send.at[base], f_recv.at[base], m, b - 1, w)

        @pl.when(down)
        def _():
            start_to(ref.at[it, 1], ref.at[it, 0], f_send.at[base + 1], f_recv.at[base + 1], m, b + 1, w)

    def halo_wait(ref, it, which):
        base = 4 * it + 2 * which

        @pl.when(down)
        def _():
            drain(ref.at[it, 2], f_recv.at[base])

        @pl.when(up)
        def _():
            drain(ref.at[it, 0], f_recv.at[base + 1])

    my_edges = eh.at[my_piece]

    def send_edges():
        for i in range(vp):

            @pl.when(down)
            def _():
                drain(eh.at[0, 1], g_recv.at[0])

            @pl.when(up)
            def _():
                drain(eh.at[0, 0], g_recv.at[1])

        start_to(my_edges, my_edges, k2_send.at[0], k2_recv.at[0], m, b, other)
        for k in order:
            start_to(my_edges, my_edges, y2_send.at[k], y2_recv.at[k], m, b, lax.rem(w + 2 * k, nw))

    def pass_edges():
        for k in reversed(order):
            piece = eh.at[pl.ds(lax.rem(w - 2 * k + nw, nw) * vp, vp)]
            drain(piece, y2_recv.at[k])
            start_to(piece, piece, k2_send.at[k], k2_recv.at[k], m, b, other)

    def rows_of(ref, first_row, stride, g):
        return ref[pl.ds(g * LB * stride + first_row, LB, stride=stride), :]

    def beside(x, y, to_left):
        shift, end = (1, lane == 0) if to_left else (LANES - 1, lane == LANES - 1)
        return jnp.where(end, pltpu.roll(y, shift, 2), pltpu.roll(x, shift, 2))

    def masked(x, depth):
        n = x.shape[0]
        return jnp.concatenate([x[:depth] * up_f, x[depth : n - depth], x[n - depth :] * down_f], axis=0)

    def smooth_group(g):
        main = [r_far[0, pl.ds(2 * LB * g + r, LB, stride=2), :] for r in range(2)]
        main += [bh[0, pl.ds(2 * LB * g + r, LB, stride=2), :] for r in range(2)]
        main += [rows_of(b1, r, LB, g) for r in range(LB)]
        main += [bh[1, pl.ds(2 * LB * g + r, LB, stride=2), :] for r in range(2)]
        main += [r_far[1, pl.ds(2 * LB * g + r, LB, stride=2), :] for r in range(2)]
        places = [(rxc, 0, 4), (rxc, 0, 5), (rx, 1, 0), (rx, 1, 1)]
        places += [(rx, 0, r) for r in range(LB)]
        places += [(rx, 1, 2), (rx, 1, 3), (rxc, 1, 2), (rxc, 1, 3)]
        sides = []
        for ref, which, r in places:
            at = 4 * (groups * r + g)
            lo, hi = (ref[which, 0], ref[which, 1]) if ref is rxc else (ref[0, which], ref[1, which])
            from_left = pltpu.roll(lo, LANES - 4 - at, 1)
            from_right = pltpu.roll(hi, (LANES - at) % LANES, 1)
            sides.append(jnp.where(lane < 4, from_right, jnp.where(lane >= LANES - 4, from_left, 0.0)))
        f0, f1 = jnp.stack(main, axis=0), jnp.stack(sides, axis=0)
        for depth in (3, 2, 1, 0):
            m0, m1 = f0[1:-1], f1[1:-1]
            n0 = beside(m0, m1, True) + beside(m0, m1, False) + f0[2:] + f0[:-2]
            n1 = beside(m1, m0, True) + beside(m1, m0, False) + f1[2:] + f1[:-2]
            f0 = CENTER * m0 + KAPPA * n0
            f1 = CENTER * m1 + KAPPA * n1
            if depth:
                f0, f1 = masked(f0, depth), masked(f1, depth)
        for r in range(LB):
            sq[pl.ds(LB * LB * g + r, LB, stride=LB), :] = f0[r]

    def member_rows(j):
        return pl.ds(pl.multiple_of(LB * j, LB), LB)

    def fourfold(x, from_row):
        x = jnp.where((row == from_row) | (row == from_row + 1), x, 0.0)
        x = x + pltpu.roll(x, 2, 1)
        return x + pltpu.roll(x, 4, 1)

    def edge_rows(gradient):
        out = []
        for side, part in enumerate((gradient[:, :LB], gradient[:, 2 * LB :])):
            tile = fourfold(part, 0 if side else LB - 2)
            rows = eh[:, side].reshape(NV, groups * 2, LB, LANES)
            out.append(jnp.sum(rows * tile[:, None], axis=0).reshape(2 * members, LANES))
        return out

    for it in range(ITERS):
        if it > 0:
            total = jnp.zeros((NV, LB, LANES), F32)
            drain(rx.at[1], h_recv.at[0])
            drain(rx.at[0], h_recv.at[1])

            @pl.when(down)
            def _():
                drain(rxc.at[1, 1], h_recv.at[2])
                drain(rxc.at[1, 0], h_recv.at[3])

            @pl.when(up)
            def _():
                drain(rxc.at[0, 1], h_recv.at[4])
                drain(rxc.at[0, 0], h_recv.at[5])

            def add_member(j, total):
                return total + et[:, j] * sq[member_rows(j), :][None]

            for g in range(groups):
                part = pl.ds(2 * LB * g, 2 * LB)

                @pl.when(down)
                def _():
                    drain(r_far.at[1, part], h_recv.at[6 + 2 * g])

                @pl.when(up)
                def _():
                    drain(r_far.at[0, part], h_recv.at[7 + 2 * g])

                smooth_group(g)
                total = lax.fori_loop(LB * g, LB * (g + 1), add_member, total, unroll=True)
            fstate[it, 1] = KEEP * fstate[it - 1, 1] - (DESCENT * scale) * total

        if it > 0:
            halo(fstate, it, 0)

        @pl.when(before)
        def _():
            start_to(
                fstate.at[it, 1], inc_next.at[it], w_send.at[2 * it], w_recv.at[2 * it], m, b, w - 1
            )

        if it == ITERS - 1:
            inc_out[0] = fstate[it, 1]
        else:
            send_edges()

            @pl.when(up)
            def _():
                drain(dif.at[0], d_recv.at[1])

            @pl.when(down)
            def _():
                drain(dif.at[2], d_recv.at[0])

        halo_wait(fstate, it, 0)
        coeff = wide(dif)

        def forth(k, u):
            moved = u + coeff * second(u) + mixed(u, False)
            moved = jnp.where(inside24, moved, 0.0)
            return jnp.where(k < count, moved, u)

        state = lax.fori_loop(0, KMAX, forth, wide(fstate.at[it]))
        ends = state[:, LB : 2 * LB]
        for part in range(3):
            ends_own[it, part] = state[:, LB * part : LB * (part + 1)]

        @pl.when(after)
        def _():
            start_to(
                ends_own.at[it],
                ends_prev.at[it],
                w_send.at[2 * it + 1],
                w_recv.at[2 * it + 1],
                m,
                b,
                w + 1,
            )

        @pl.when(after)
        def _():
            drain(inc_next.at[it], w_recv.at[2 * it])

        dense = wv[...].reshape(2, NV, LB, LANES)
        to_next = jnp.where(after, ewb[...] * (ends - inc_next[it]), 0.0)
        bstate[it, 1] = dense[0] * ends - dense[1] + to_next
        halo(bstate, it, 1)
        if it == 0:
            pass_edges()
        halo_wait(bstate, it, 1)

        def back(k, y):
            moved = y + second(coeff * y) + mixed(y, True)
            moved = jnp.where(inside24, moved, 0.0)
            return jnp.where(KMAX - 1 - k < count, moved, y)

        state = lax.fori_loop(0, KMAX, back, wide(bstate.at[it]))

        @pl.when(before)
        def _():
            drain(ends_prev.at[it], w_recv.at[2 * it + 1])

        wide_w = jnp.concatenate([ewb[...]] * 3, axis=1)
        misfit = jnp.where(before, wide_w * (wide(ends_prev.at[it]) - wide(fstate.at[it])), 0.0)
        gradient = (state - misfit) * scale
        own = gradient[:, LB : 2 * LB]

        if it == 0:

            def spread(j, _):
                b1[member_rows(j), :] = jnp.sum(et[:, j] * own, axis=0)
                return 0

            lax.fori_loop(0, members, spread, 0, unroll=4)
            for g in range(groups):
                for r in range(2):
                    to_row = pl.ds(2 * LB * g + r, LB, stride=2)
                    b_up[to_row, :] = rows_of(b1, 2 + r, LB, g)
                    b_down[to_row, :] = rows_of(b1, 4 + r, LB, g)

            for k in range(planes):
                drain(my_edges, k2_recv.at[k])
            top, bottom = edge_rows(gradient)
            bh[0] = top
            bh[1] = bottom
            for part in range(2):
                lo = hi = jnp.zeros((LB, LANES), F32)
                for r in range(LB if part == 0 else 4):
                    for g in range(groups):
                        if part == 0:
                            x = rows_of(b1, r, LB, g)
                        else:
                            x = bh[r // 2, pl.ds(2 * LB * g + r % 2, LB, stride=2), :]
                        at = groups * r + g
                        here = lax.shift_right_logical(lane, 2) == at
                        lo = jnp.where(here, pltpu.roll(x, 4 * at, 1) if at else x, lo)
                        hi = jnp.where(here, pltpu.roll(x, (4 * at + 4) % LANES, 1), hi)
                pk[0, part] = lo
                pk[1, part] = hi

            @pl.when(up)
            def _():
                start_to(pk.at[0, 0], rxc.at[1, 1], h_send.at[2], h_recv.at[2], left, b - 1, w)
                start_to(pk.at[1, 0], rxc.at[1, 0], h_send.at[3], h_recv.at[3], right, b - 1, w)

            @pl.when(down)
            def _():
                start_to(pk.at[0, 0], rxc.at[0, 1], h_send.at[4], h_recv.at[4], left, b + 1, w)
                start_to(pk.at[1, 0], rxc.at[0, 0], h_send.at[5], h_recv.at[5], right, b + 1, w)

            start_to(pk.at[0], rx.at[1], h_send.at[0], h_recv.at[0], left, b, w)
            start_to(pk.at[1], rx.at[0], h_send.at[1], h_recv.at[1], right, b, w)
            for g in range(groups):
                part = pl.ds(2 * LB * g, 2 * LB)

                @pl.when(up)
                def _():
                    start_to(
                        b_up.at[part], r_far.at[1, part], h_send.at[6 + 2 * g], h_recv.at[6 + 2 * g], m, b - 1, w
                    )

                @pl.when(down)
                def _():
                    start_to(
                        b_down.at[part], r_far.at[0, part], h_send.at[7 + 2 * g], h_recv.at[7 + 2 * g], m, b + 1, w
                    )
        else:

            def gather(q, _):
                for i in range(2):
                    j = 2 * q + i
                    x = jnp.sum(et[:, j] * own, axis=0)
                    obuf[q, i] = (KEEP * DESCENT) * b1[member_rows(j), :] + DESCENT * x
                return 0

            lax.fori_loop(0, nm, gather, 0, unroll=2)
            top, bottom = edge_rows(gradient)
            top = (KEEP * DESCENT) * bh[0] + DESCENT * top
            bottom = (KEEP * DESCENT) * bh[1] + DESCENT * bottom
            for q in range(nm):
                obuf[q, 2, 0:4] = top[4 * q : 4 * q + 4]
                obuf[q, 2, 4:8] = bottom[4 * q : 4 * q + 4]

    c_in[:, :, mine] = obuf[m]

    def send_o(k, _):
        to = lax.rem(m + k, nm)
        start_to(obuf.at[to], c_in.at[:, :, mine], o_send, o_recv, to, b, w)
        return 0

    lax.fori_loop(1, nm, send_o, 0)
    drain(obuf.at[pl.ds(0, nm - 1)], o_recv)
    packed = c_in[2]
    for i in range(2):
        h = smooth_twice(c_in[i], packed, i)
        ctl_out[0, i] = (KEEP * KEEP) * cbuf[i] - h

    for i in range(vp):
        drain(et.at[0, pl.ds(0, members - 2)], e_send)
    for k in range(planes):
        drain(et.at[my_piece], k_send.at[k])
        drain(my_edges, k2_send.at[k])
        if k > 0:
            drain(et.at[my_piece], y_send.at[k])
            drain(my_edges, y2_send.at[k])
    drain(s_in.at[pl.ds(0, members - 2)], s_send.at[0])
    drain(obuf.at[pl.ds(0, nm - 1)], o_send)

    @pl.when(up)
    def _():
        drain(s_top, s_send.at[1])
        drain(dif.at[1], d_send.at[0])
        drain(e_up, g_send.at[0])
        drain(pk.at[0, 0], h_send.at[2])
        drain(pk.at[1, 0], h_send.at[3])
        for it in range(ITERS):
            drain(fstate.at[it, 1], f_send.at[4 * it])
            drain(bstate.at[it, 1], f_send.at[4 * it + 2])

    @pl.when(down)
    def _():
        drain(s_bot, s_send.at[2])
        drain(dif.at[1], d_send.at[1])
        drain(e_down, g_send.at[1])
        drain(pk.at[0, 0], h_send.at[4])
        drain(pk.at[1, 0], h_send.at[5])
        for it in range(ITERS):
            drain(fstate.at[it, 1], f_send.at[4 * it + 1])
            drain(bstate.at[it, 1], f_send.at[4 * it + 3])

    drain(pk.at[0], h_send.at[0])
    drain(pk.at[1], h_send.at[1])
    for g in range(groups):
        part = pl.ds(2 * LB * g, 2 * LB)

        @pl.when(up)
        def _():
            drain(b_up.at[part], h_send.at[6 + 2 * g])

        @pl.when(down)
        def _():
            drain(b_down.at[part], h_send.at[7 + 2 * g])

    for it in range(ITERS):

        @pl.when(before)
        def _():
            drain(fstate.at[it, 1], w_send.at[2 * it])

        @pl.when(after)
        def _():
            drain(ends_own.at[it], w_send.at[2 * it + 1])


def local_part(nm, nl, nw, *args):
    (
        ensemble,
        weights,
        diffusivity,
        coupling,
        tl_steps,
        obs_cell,
        obs_window,
        obs_value,
        obs_weight,
        error_weight,
    ) = args
    members = 2 * nm
    lon = nm * LANES
    planes = nw // 2
    groups = members // LB
    anywhere = pl.BlockSpec(memory_space=pltpu.HBM)
    obs = [x.reshape(-1, LANES) for x in (obs_cell, obs_window, obs_value, obs_weight)]
    tile = (LB, LANES)
    state = (NV, *tile)

    def buf(*shape):
        return pltpu.VMEM(shape, F32)

    dma = pltpu.SemaphoreType.DMA
    return pl.pallas_call(
        functools.partial(kernel, nm, nl, nw),
        name="assimilate",
        out_shape=(
            pltpu.VMEM((1, 2, LB, lon), F32),
            pltpu.VMEM((1, *state), F32),
        ),
        in_specs=[anywhere] * 4 + [pl.BlockSpec(memory_space=pltpu.SMEM)] + [anywhere] * 5,
        out_specs=(pl.BlockSpec(memory_space=pltpu.VMEM),)*2,
        scratch_shapes=[
            pltpu.SMEM((NV, NV), F32),
            pltpu.SMEM((NV,), F32),
            pltpu.VMEM(obs[0].shape, jnp.int32),
            pltpu.VMEM(obs[0].shape, jnp.int32),
            buf(*obs[0].shape),
            buf(*obs[0].shape),
            buf(NV, members, *tile),
            buf(2, LB, lon),
            buf(2, LB, lon),
            buf(4, lon),
            buf(4, lon),
            buf(members, *tile),
            buf(4, lon),
            buf(4, lon),
            buf(3, *state),
            buf(ITERS, 3, *state),
            buf(ITERS, 3, *state),
            buf(ITERS, *state),
            buf(ITERS, 3, *state),
            buf(ITERS, 3, *state),
            buf(2 * NV * LB, LANES),
            buf(*state),
            buf(2 * members, LANES),
            buf(2 * members, LANES),
            buf(NV, 2, 2 * members, LANES),
            buf(members * LB, LANES),
            buf(2, 2 * members, LANES),
            buf(2 * members, LANES),
            buf(2 * members, LANES),
            buf(2, 2 * members, LANES),
            buf(2, 2, *tile),
            buf(2, 2, *tile),
            buf(2, 2, *tile),
            buf(members * LB, LANES),
            buf(nm, 3, *tile),
            buf(3, LB, lon),
            dma((12,)),
            dma,
            dma,
            dma((planes,)),
            dma((planes,)),
            dma((planes,)),
            dma((planes,)),
            dma((3,)),
            dma((3,)),
            dma((2,)),
            dma((2,)),
            dma((4 * ITERS,)),
            dma((4 * ITERS,)),
            dma((2 * ITERS,)),
            dma((2 * ITERS,)),
            dma((2,)),
            dma((2,)),
            dma((planes,)),
            dma((planes,)),
            dma((planes,)),
            dma((planes,)),
            dma((2 * groups + 6,)),
            dma((2 * groups + 6,)),
            dma,
            dma,
        ],
        compiler_params=pltpu.CompilerParams(
            collective_id=0, has_side_effects=True, vmem_limit_bytes=40 * 1024 * 1024
        ),
    )(
        *(pltpu.with_memory_space_constraint(x, pltpu.HBM) for x in (ensemble, weights, diffusivity, coupling)),
        tl_steps,
        *(pltpu.with_memory_space_constraint(x, pltpu.HBM) for x in (*obs, error_weight)),
    )


def solution(mesh):
    sizes = [mesh.shape[axis] for axis in ("mem", "lat", "win")]
    return jax.shard_map(
        functools.partial(local_part, *sizes),
        mesh=mesh,
        in_specs=(
            P("mem", None, "lat", None),
            P("win", "mem", "lat", None),
            P(None, "lat", "mem"),
            P(),
            P("win"),
            P(("mem", "lat")),
            P(("mem", "lat")),
            P(("mem", "lat")),
            P(("mem", "lat")),
            P(),
        ),
        out_specs=(P("win", "mem", "lat", None), P("win", None, "lat", "mem")),
        check_vma=False,
    )
```

```python
import functools
import math

import jax
import jax.numpy as jnp
from jax import lax
from jax.experimental import pallas as pl
from jax.experimental.pallas import tpu as pltpu
from jax.sharding import PartitionSpec as P

MESH = pl.DeviceIdType.MESH
NV = 8
LB = 8
LANES = 128
KMAX = 6
ITERS = 2
KAPPA = 0.125
DESCENT = 0.25
KEEP = 1.0 - DESCENT
CENTER = 1.0 - 4.0 * KAPPA
F32 = jnp.float32


def start_to(src, dst, send_sem, recv_sem, mem, lat, win):
    pltpu.make_async_remote_copy(
        src_ref=src,
        dst_ref=dst,
        send_sem=send_sem,
        recv_sem=recv_sem,
        device_id={"mem": mem, "lat": lat, "win": win},
        device_id_type=MESH,
    ).start()


def drain(ref, sem):
    pltpu.make_async_copy(ref, ref, sem).wait()


def along(f, lon):
    return CENTER * f + KAPPA * (pltpu.roll(f, 1, 1) + pltpu.roll(f, lon - 1, 1))


def kernel(
    nm,
    nl,
    nw,
    e_hbm,
    c_hbm,
    d_hbm,
    coup_hbm,
    steps,
    obs0,
    obs1,
    obs2,
    obs3,
    err_hbm,
    ctl_out,
    inc_out,
    coup,
    err_w,
    obs_cell,
    obs_window,
    obs_value,
    obs_weight,
    et,
    cbuf,
    sm,
    s_top,
    s_bot,
    s_in,
    r_top,
    r_bot,
    dif,
    fstate,
    bstate,
    inc_next,
    ends_own,
    ends_prev,
    wv,
    ewb,
    e_up,
    e_down,
    eh,
    b1,
    bh,
    b_up,
    b_down,
    r_far,
    pk,
    rx,
    rxc,
    sq,
    obuf,
    c_in,
    local,
    e_send,
    e_recv,
    y_send,
    y_recv,
    k_send,
    k_recv,
    s_send,
    s_recv,
    d_send,
    d_recv,
    f_send,
    f_recv,
    w_send,
    w_recv,
    g_send,
    g_recv,
    y2_send,
    y2_recv,
    k2_send,
    k2_recv,
    h_send,
    h_recv,
    o_send,
    o_recv,
):
    m, b, w = lax.axis_index("mem"), lax.axis_index("lat"), lax.axis_index("win")
    members = 2 * nm
    lon = nm * LANES
    vp = NV // nw
    scale = 1.0 / math.sqrt(members - 1)
    up, down = b > 0, b < nl - 1
    before, after = w > 0, w < nw - 1
    other = w + 1 - 2 * lax.rem(w, 2)
    planes = nw // 2
    groups = members // LB
    left, right = lax.rem(m + nm - 1, nm), lax.rem(m + 1, nm)
    mine = pl.ds(pl.multiple_of(m * LANES, LANES), LANES)
    my_pair = pl.ds(2 * m, 2)
    my_piece = pl.ds(w * vp, vp)

    load_c = pltpu.make_async_copy(c_hbm.at[0], cbuf, local.at[0])
    load_c.start()
    load_d = pltpu.make_async_copy(d_hbm, dif.at[1], local.at[1])
    load_d.start()
    small = [
        pltpu.make_async_copy(src, dst, local.at[5 + i])
        for i, (src, dst) in enumerate(
            (
                (coup_hbm, coup),
                (err_hbm, err_w),
                (obs0, obs_cell),
                (obs1, obs_window),
                (obs2, obs_value),
                (obs3, obs_weight),
            )
        )
    ]
    for copy in small:
        copy.start()
    for i in range(vp):
        pltpu.make_async_copy(
            e_hbm.at[:, w * vp + i, :, mine], et.at[w * vp + i, my_pair], local.at[2]
        ).start()

    barrier = pltpu.get_barrier_semaphore()

    def hello(mem, lat, win):
        pl.semaphore_signal(
            barrier, inc=1, device_id={"mem": mem, "lat": lat, "win": win}, device_id_type=MESH
        )

    def greet(k, _):
        hello(lax.rem(m + k, nm), b, w)
        return 0

    lax.fori_loop(1, nm, greet, 0, unroll=True)

    @pl.when(up)
    def _():
        hello(m, b - 1, w)

    @pl.when(down)
    def _():
        hello(m, b + 1, w)

    for k in range(1, planes):
        hello(m, b, lax.rem(w + 2 * k, nw))
    hello(m, b, other)
    odd = lax.rem(w, 2)

    @pl.when((odd == 0) & before)
    def _():
        hello(m, b, w - 1)

    @pl.when((odd == 1) & after)
    def _():
        hello(m, b, w + 1)

    one_more = jnp.where((w > 0) & (w < nw - 1), 1, 0)
    bands = jnp.where(up, 1, 0) + jnp.where(down, 1, 0)

    load_c.wait()
    row8 = lax.broadcasted_iota(jnp.int32, (LB, lon), 0)
    first, last = row8 == 0, row8 == LB - 1
    edge = jnp.where(first & up, 1.0, 0.0) + jnp.where(last & down, 1.0, 0.0)
    packed = jnp.where(row8 < 2, cbuf[0], cbuf[1])
    packed = jnp.where((row8 == 2) | (row8 == 3), pltpu.roll(cbuf[1], 2, 0), packed)
    packed = jnp.where((row8 == 4) | (row8 == 5), pltpu.roll(cbuf[0], LB - 2, 0), packed)
    s_top[...] = packed[0:4]
    s_bot[...] = packed[4:8]
    pl.semaphore_wait(barrier, nm - 1 + bands + planes + one_more)

    @pl.when(up)
    def _():
        start_to(s_top, r_bot, s_send.at[1], s_recv.at[1], m, b - 1, w)

    @pl.when(down)
    def _():
        start_to(s_bot, r_top, s_send.at[2], s_recv.at[2], m, b + 1, w)

    def send_e(k, _):
        to = lax.rem(m + k, nm)
        for i in range(vp):
            start_to(
                e_hbm.at[:, w * vp + i, :, pl.ds(pl.multiple_of(to * LANES, LANES), LANES)],
                et.at[w * vp + i, my_pair],
                e_send,
                e_recv,
                to,
                b,
                w,
            )
        return 0

    lax.fori_loop(1, nm, send_e, 0, unroll=True)

    @pl.when(jnp.logical_not(up))
    def _():
        dif[0] = jnp.zeros_like(dif[0])
        r_top[...] = jnp.zeros_like(r_top)
        r_far[0] = jnp.zeros_like(r_far[0])
        rxc[0] = jnp.zeros_like(rxc[0])
        for i in range(vp):
            eh[w * vp + i, 0] = jnp.zeros_like(r_far[0])
        for it in range(ITERS):
            fstate[it, 0] = jnp.zeros_like(fstate[it, 0])
            bstate[it, 0] = jnp.zeros_like(bstate[it, 0])

    @pl.when(jnp.logical_not(down))
    def _():
        dif[2] = jnp.zeros_like(dif[2])
        r_bot[...] = jnp.zeros_like(r_bot)
        r_far[1] = jnp.zeros_like(r_far[1])
        rxc[1] = jnp.zeros_like(rxc[1])
        for i in range(vp):
            eh[w * vp + i, 1] = jnp.zeros_like(r_far[1])
        for it in range(ITERS):
            fstate[it, 2] = jnp.zeros_like(fstate[it, 2])
            bstate[it, 2] = jnp.zeros_like(bstate[it, 2])

    @pl.when(jnp.logical_not(before))
    def _():
        ends_prev[...] = jnp.zeros_like(ends_prev)

    @pl.when(jnp.logical_not(after))
    def _():
        inc_next[...] = jnp.zeros_like(inc_next)

    for copy in small:
        copy.wait()
    for v in range(NV):
        ewb[v] = jnp.full((LB, LANES), err_w[v], F32)

    tall = lax.broadcasted_iota(jnp.int32, (NV * LB, LANES), 0)
    lane_of = lax.broadcasted_iota(jnp.int32, (LANES, LANES), 0)

    def add_obs(k, total):
        at = pl.ds(k, 1)
        cell = obs_cell[at, :]
        here = (tall == lax.shift_right_logical(cell, 7)) & (obs_window[at, :] == w)
        weight = jnp.where(here, obs_weight[at, :], 0.0)
        both = jnp.concatenate([weight, weight * obs_value[at, :]], axis=0)
        hot = jnp.where(lane_of == (cell & (LANES - 1)), 1.0, 0.0)
        return total + lax.dot_general(
            both,
            hot,
            (((1,), (1,)), ((), ())),
            precision=lax.Precision.HIGHEST,
            preferred_element_type=F32,
        )

    wv[...] = lax.fori_loop(
        0, obs_cell.shape[0], add_obs, jnp.zeros((2 * NV * LB, LANES), F32)
    )

    def smooth_twice(f, packed, i):
        near = jnp.where(
            first,
            pltpu.roll(packed, LB - (2 * i + 1), 0),
            pltpu.roll(packed, 3 - 2 * i, 0),
        )
        far = jnp.where(
            first,
            pltpu.roll(packed, LB - 2, 0) if i else packed,
            packed if i else pltpu.roll(packed, 2, 0),
        )
        g = along(f, lon) + KAPPA * (
            jnp.where(first, near, pltpu.roll(f, 1, 0)) + jnp.where(last, near, pltpu.roll(f, LB - 1, 0))
        )
        e1 = (along(near, lon) + KAPPA * (far + f)) * edge
        return along(g, lon) + KAPPA * (
            jnp.where(first, e1, pltpu.roll(g, 1, 0)) + jnp.where(last, e1, pltpu.roll(g, LB - 1, 0))
        )

    @pl.when(up)
    def _():
        drain(r_top, s_recv.at[2])

    @pl.when(down)
    def _():
        drain(r_bot, s_recv.at[1])

    packed = jnp.concatenate([r_top[...], r_bot[...]], axis=0)
    for i in range(2):
        sm[i] = smooth_twice(cbuf[i], packed, i)

    def send_s(k, _):
        to = lax.rem(m + k, nm)
        cut = pl.ds(pl.multiple_of(to * LANES, LANES), LANES)
        start_to(sm.at[:, :, cut], s_in.at[my_pair], s_send.at[0], s_recv.at[0], to, b, w)
        return 0

    lax.fori_loop(1, nm, send_s, 0, unroll=True)
    for i in range(vp):
        drain(et.at[w * vp + i, my_pair], local.at[2])
        drain(et.at[0, pl.ds(0, members - 2)], e_recv)
    start_to(et.at[my_piece], et.at[my_piece], k_send.at[0], k_recv.at[0], m, b, other)
    order = sorted(range(1, planes), key=lambda k: -min(k, planes - k))
    for k in order:
        start_to(
            et.at[my_piece], et.at[my_piece], y_send.at[k], y_recv.at[k], m, b, lax.rem(w + 2 * k, nw)
        )
    s_in[my_pair] = sm[:, :, mine]
    drain(s_in.at[pl.ds(0, members - 2)], s_recv.at[0])
    load_d.wait()

    @pl.when(up)
    def _():
        start_to(dif.at[1], dif.at[2], d_send.at[0], d_recv.at[0], m, b - 1, w)

    @pl.when(down)
    def _():
        start_to(dif.at[1], dif.at[0], d_send.at[1], d_recv.at[1], m, b + 1, w)


    def first_increment(v):
        fstate[0, 1, v] = jnp.sum(et[v] * s_in[...], axis=0) * scale

        @pl.when(up)
        def _():
            start_to(fstate.at[0, 1, v], fstate.at[0, 2, v], f_send.at[0], f_recv.at[0], m, b - 1, w)

        @pl.when(down)
        def _():
            start_to(fstate.at[0, 1, v], fstate.at[0, 0, v], f_send.at[1], f_recv.at[1], m, b + 1, w)

    for i in range(vp):
        v = w * vp + i
        for j in range(members):
            e_up[2 * j : 2 * j + 2, :] = et[v, j, 0:2]
            e_down[2 * j : 2 * j + 2, :] = et[v, j, 6:8]

        @pl.when(up)
        def _():
            start_to(e_up, eh.at[v, 1], g_send.at[0], g_recv.at[0], m, b - 1, w)

        @pl.when(down)
        def _():
            start_to(e_down, eh.at[v, 0], g_send.at[1], g_recv.at[1], m, b + 1, w)

        if i < vp - 1:

            @pl.when(up)
            def _():
                drain(e_up, g_send.at[0])

            @pl.when(down)
            def _():
                drain(e_down, g_send.at[1])

        first_increment(v)

    for k in reversed(order):
        origin = lax.rem(w - 2 * k + nw, nw) * vp
        piece = et.at[pl.ds(origin, vp)]
        drain(piece, y_recv.at[k])
        start_to(piece, piece, k_send.at[k], k_recv.at[k], m, b, other)
        for i in range(vp):
            first_increment(origin + i)
    for k in [0, *reversed(order)]:
        origin = lax.rem(other - 2 * k + nw, nw) * vp
        drain(et.at[pl.ds(origin, vp)], k_recv.at[k])
        for i in range(vp):
            first_increment(origin + i)

    rows24 = lax.broadcasted_iota(jnp.int32, (3 * LB, LANES), 0)
    inside24 = ((rows24 >= LB) | up) & ((rows24 < 2 * LB) | down)
    lane = lax.broadcasted_iota(jnp.int32, (LB, LANES), 1)
    row = lax.broadcasted_iota(jnp.int32, (LB, LANES), 0)
    up_f = jnp.where(up, 1.0, 0.0)
    down_f = jnp.where(down, 1.0, 0.0)

    def wide(ref):
        return jnp.concatenate([ref[0], ref[1], ref[2]], axis=1)

    def second(x):
        return pltpu.roll(x, 1, 1) + pltpu.roll(x, 3 * LB - 1, 1) - 2.0 * x

    def mixed(x, transposed):
        rows = []
        for v in range(NV):
            total = None
            for u in range(NV):
                term = (coup[u, v] if transposed else coup[v, u]) * x[u]
                total = term if total is None else total + term
            rows.append(total)
        return jnp.stack(rows, axis=0)

    count = jnp.full((3 * LB, LANES), steps[0], jnp.int32)

    def halo(ref, it, which):
        base = 4 * it + 2 * which

        @pl.when(up)
        def _():
            start_to(ref.at[it, 1], ref.at[it, 2], f_send.at[base], f_recv.at[base], m, b - 1, w)

        @pl.when(down)
        def _():
            start_to(ref.at[it, 1], ref.at[it, 0], f_send.at[base + 1], f_recv.at[base + 1], m, b + 1, w)

    def halo_wait(ref, it, which):
        base = 4 * it + 2 * which

        @pl.when(down)
        def _():
            drain(ref.at[it, 2], f_recv.at[base])

        @pl.when(up)
        def _():
            drain(ref.at[it, 0], f_recv.at[base + 1])

    my_edges = eh.at[my_piece]

    def send_edges():
        for i in range(vp):

            @pl.when(down)
            def _():
                drain(eh.at[0, 1], g_recv.at[0])

            @pl.when(up)
            def _():
                drain(eh.at[0, 0], g_recv.at[1])

        start_to(my_edges, my_edges, k2_send.at[0], k2_recv.at[0], m, b, other)
        for k in order:
            start_to(my_edges, my_edges, y2_send.at[k], y2_recv.at[k], m, b, lax.rem(w + 2 * k, nw))

    def pass_edges():
        for k in reversed(order):
            piece = eh.at[pl.ds(lax.rem(w - 2 * k + nw, nw) * vp, vp)]
            drain(piece, y2_recv.at[k])
            start_to(piece, piece, k2_send.at[k], k2_recv.at[k], m, b, other)

    def rows_of(ref, first_row, stride, g):
        return ref[pl.ds(g * LB * stride + first_row, LB, stride=stride), :]

    def beside(x, y, to_left):
        shift, end = (1, lane == 0) if to_left else (LANES - 1, lane == LANES - 1)
        return jnp.where(end, pltpu.roll(y, shift, 2), pltpu.roll(x, shift, 2))

    def masked(x, depth):
        n = x.shape[0]
        return jnp.concatenate([x[:depth] * up_f, x[depth : n - depth], x[n - depth :] * down_f], axis=0)

    def smooth_group(g):
        main = [r_far[0, pl.ds(2 * LB * g + r, LB, stride=2), :] for r in range(2)]
        main += [bh[0, pl.ds(2 * LB * g + r, LB, stride=2), :] for r in range(2)]
        main += [rows_of(b1, r, LB, g) for r in range(LB)]
        main += [bh[1, pl.ds(2 * LB * g + r, LB, stride=2), :] for r in range(2)]
        main += [r_far[1, pl.ds(2 * LB * g + r, LB, stride=2), :] for r in range(2)]
        places = [(rxc, 0, 4), (rxc, 0, 5), (rx, 1, 0), (rx, 1, 1)]
        places += [(rx, 0, r) for r in range(LB)]
        places += [(rx, 1, 2), (rx, 1, 3), (rxc, 1, 2), (rxc, 1, 3)]
        sides = []
        for ref, which, r in places:
            at = 4 * (groups * r + g)
            lo, hi = (ref[which, 0], ref[which, 1]) if ref is rxc else (ref[0, which], ref[1, which])
            from_left = pltpu.roll(lo, LANES - 4 - at, 1)
            from_right = pltpu.roll(hi, (LANES - at) % LANES, 1)
            sides.append(jnp.where(lane < 4, from_right, jnp.where(lane >= LANES - 4, from_left, 0.0)))
        f0, f1 = jnp.stack(main, axis=0), jnp.stack(sides, axis=0)
        for depth in (3, 2, 1, 0):
            m0, m1 = f0[1:-1], f1[1:-1]
            n0 = beside(m0, m1, True) + beside(m0, m1, False) + f0[2:] + f0[:-2]
            n1 = beside(m1, m0, True) + beside(m1, m0, False) + f1[2:] + f1[:-2]
            f0 = CENTER * m0 + KAPPA * n0
            f1 = CENTER * m1 + KAPPA * n1
            if depth:
                f0, f1 = masked(f0, depth), masked(f1, depth)
        for r in range(LB):
            sq[pl.ds(LB * LB * g + r, LB, stride=LB), :] = f0[r]

    def member_rows(j):
        return pl.ds(pl.multiple_of(LB * j, LB), LB)

    def fourfold(x, from_row):
        x = jnp.where((row == from_row) | (row == from_row + 1), x, 0.0)
        x = x + pltpu.roll(x, 2, 1)
        return x + pltpu.roll(x, 4, 1)

    def edge_rows(gradient):
        out = []
        for side, part in enumerate((gradient[:, :LB], gradient[:, 2 * LB :])):
            tile = fourfold(part, 0 if side else LB - 2)
            rows = eh[:, side].reshape(NV, groups * 2, LB, LANES)
            out.append(jnp.sum(rows * tile[:, None], axis=0).reshape(2 * members, LANES))
        return out

    for it in range(ITERS):
        if it > 0:
            total = jnp.zeros((NV, LB, LANES), F32)
            drain(rx.at[1], h_recv.at[0])
            drain(rx.at[0], h_recv.at[1])

            @pl.when(down)
            def _():
                drain(rxc.at[1, 1], h_recv.at[2])
                drain(rxc.at[1, 0], h_recv.at[3])

            @pl.when(up)
            def _():
                drain(rxc.at[0, 1], h_recv.at[4])
                drain(rxc.at[0, 0], h_recv.at[5])

            def add_member(j, total):
                return total + et[:, j] * sq[member_rows(j), :][None]

            for g in range(groups):
                part = pl.ds(2 * LB * g, 2 * LB)

                @pl.when(down)
                def _():
                    drain(r_far.at[1, part], h_recv.at[6 + 2 * g])

                @pl.when(up)
                def _():
                    drain(r_far.at[0, part], h_recv.at[7 + 2 * g])

                smooth_group(g)
                total = lax.fori_loop(LB * g, LB * (g + 1), add_member, total, unroll=True)
            fstate[it, 1] = KEEP * fstate[it - 1, 1] - (DESCENT * scale) * total

        if it > 0:
            halo(fstate, it, 0)

        @pl.when(before)
        def _():
            start_to(
                fstate.at[it, 1], inc_next.at[it], w_send.at[2 * it], w_recv.at[2 * it], m, b, w - 1
            )

        if it == ITERS - 1:
            inc_out[0] = fstate[it, 1]
        else:
            send_edges()

            @pl.when(up)
            def _():
                drain(dif.at[0], d_recv.at[1])

            @pl.when(down)
            def _():
                drain(dif.at[2], d_recv.at[0])

        halo_wait(fstate, it, 0)
        coeff = wide(dif)

        def forth(k, u):
            moved = u + coeff * second(u) + mixed(u, False)
            moved = jnp.where(inside24, moved, 0.0)
            return jnp.where(k < count, moved, u)

        state = lax.fori_loop(0, KMAX, forth, wide(fstate.at[it]))
        ends = state[:, LB : 2 * LB]
        for part in range(3):
            ends_own[it, part] = state[:, LB * part : LB * (part + 1)]

        @pl.when(after)
        def _():
            start_to(
                ends_own.at[it],
                ends_prev.at[it],
                w_send.at[2 * it + 1],
                w_recv.at[2 * it + 1],
                m,
                b,
                w + 1,
            )

        @pl.when(after)
        def _():
            drain(inc_next.at[it], w_recv.at[2 * it])

        dense = wv[...].reshape(2, NV, LB, LANES)
        to_next = jnp.where(after, ewb[...] * (ends - inc_next[it]), 0.0)
        bstate[it, 1] = dense[0] * ends - dense[1] + to_next
        halo(bstate, it, 1)
        if it == 0:
            pass_edges()
        halo_wait(bstate, it, 1)

        def back(k, y):
            moved = y + second(coeff * y) + mixed(y, True)
            moved = jnp.where(inside24, moved, 0.0)
            return jnp.where(KMAX - 1 - k < count, moved, y)

        state = lax.fori_loop(0, KMAX, back, wide(bstate.at[it]))

        @pl.when(before)
        def _():
            drain(ends_prev.at[it], w_recv.at[2 * it + 1])

        wide_w = jnp.concatenate([ewb[...]] * 3, axis=1)
        misfit = jnp.where(before, wide_w * (wide(ends_prev.at[it]) - wide(fstate.at[it])), 0.0)
        gradient = (state - misfit) * scale
        own = gradient[:, LB : 2 * LB]

        if it == 0:

            def spread(j, _):
                b1[member_rows(j), :] = jnp.sum(et[:, j] * own, axis=0)
                return 0

            lax.fori_loop(0, members, spread, 0, unroll=4)
            for g in range(groups):
                for r in range(2):
                    to_row = pl.ds(2 * LB * g + r, LB, stride=2)
                    b_up[to_row, :] = rows_of(b1, 2 + r, LB, g)
                    b_down[to_row, :] = rows_of(b1, 4 + r, LB, g)

            def send_corners():
                @pl.when(up)
                def _():
                    start_to(pk.at[0, 0], rxc.at[1, 1], h_send.at[2], h_recv.at[2], left, b - 1, w)
                    start_to(pk.at[1, 0], rxc.at[1, 0], h_send.at[3], h_recv.at[3], right, b - 1, w)

                @pl.when(down)
                def _():
                    start_to(pk.at[0, 0], rxc.at[0, 1], h_send.at[4], h_recv.at[4], left, b + 1, w)
                    start_to(pk.at[1, 0], rxc.at[0, 0], h_send.at[5], h_recv.at[5], right, b + 1, w)

            for part in range(2):
                if part == 1:
                    send_corners()
                    for k in range(planes):
                        drain(my_edges, k2_recv.at[k])
                    top, bottom = edge_rows(gradient)
                    bh[0] = top
                    bh[1] = bottom
                lo = hi = jnp.zeros((LB, LANES), F32)
                for r in range(LB if part == 0 else 4):
                    for g in range(groups):
                        if part == 0:
                            x = rows_of(b1, r, LB, g)
                        else:
                            x = bh[r // 2, pl.ds(2 * LB * g + r % 2, LB, stride=2), :]
                        at = groups * r + g
                        here = lax.shift_right_logical(lane, 2) == at
                        lo = jnp.where(here, pltpu.roll(x, 4 * at, 1) if at else x, lo)
                        hi = jnp.where(here, pltpu.roll(x, (4 * at + 4) % LANES, 1), hi)
                pk[0, part] = lo
                pk[1, part] = hi

            start_to(pk.at[0], rx.at[1], h_send.at[0], h_recv.at[0], left, b, w)
            start_to(pk.at[1], rx.at[0], h_send.at[1], h_recv.at[1], right, b, w)
            for g in range(groups):
                part = pl.ds(2 * LB * g, 2 * LB)

                @pl.when(up)
                def _():
                    start_to(
                        b_up.at[part], r_far.at[1, part], h_send.at[6 + 2 * g], h_recv.at[6 + 2 * g], m, b - 1, w
                    )

                @pl.when(down)
                def _():
                    start_to(
                        b_down.at[part], r_far.at[0, part], h_send.at[7 + 2 * g], h_recv.at[7 + 2 * g], m, b + 1, w
                    )
        else:

            def gather(q, _):
                for i in range(2):
                    j = 2 * q + i
                    x = jnp.sum(et[:, j] * own, axis=0)
                    obuf[q, i] = (KEEP * DESCENT) * b1[member_rows(j), :] + DESCENT * x
                return 0

            lax.fori_loop(0, nm, gather, 0, unroll=2)
            top, bottom = edge_rows(gradient)
            top = (KEEP * DESCENT) * bh[0] + DESCENT * top
            bottom = (KEEP * DESCENT) * bh[1] + DESCENT * bottom
            for q in range(nm):
                obuf[q, 2, 0:4] = top[4 * q : 4 * q + 4]
                obuf[q, 2, 4:8] = bottom[4 * q : 4 * q + 4]

    c_in[:, :, mine] = obuf[m]

    def send_o(k, _):
        to = lax.rem(m + k, nm)
        start_to(obuf.at[to], c_in.at[:, :, mine], o_send, o_recv, to, b, w)
        return 0

    lax.fori_loop(1, nm, send_o, 0, unroll=True)
    drain(obuf.at[pl.ds(0, nm - 1)], o_recv)
    packed = c_in[2]
    for i in range(2):
        h = smooth_twice(c_in[i], packed, i)
        ctl_out[0, i] = (KEEP * KEEP) * cbuf[i] - h

    for i in range(vp):
        drain(et.at[0, pl.ds(0, members - 2)], e_send)
    for k in range(planes):
        drain(et.at[my_piece], k_send.at[k])
        drain(my_edges, k2_send.at[k])
        if k > 0:
            drain(et.at[my_piece], y_send.at[k])
            drain(my_edges, y2_send.at[k])
    drain(s_in.at[pl.ds(0, members - 2)], s_send.at[0])
    drain(obuf.at[pl.ds(0, nm - 1)], o_send)

    @pl.when(up)
    def _():
        drain(s_top, s_send.at[1])
        drain(dif.at[1], d_send.at[0])
        drain(e_up, g_send.at[0])
        drain(pk.at[0, 0], h_send.at[2])
        drain(pk.at[1, 0], h_send.at[3])
        for it in range(ITERS):
            drain(fstate.at[it, 1], f_send.at[4 * it])
            drain(bstate.at[it, 1], f_send.at[4 * it + 2])

    @pl.when(down)
    def _():
        drain(s_bot, s_send.at[2])
        drain(dif.at[1], d_send.at[1])
        drain(e_down, g_send.at[1])
        drain(pk.at[0, 0], h_send.at[4])
        drain(pk.at[1, 0], h_send.at[5])
        for it in range(ITERS):
            drain(fstate.at[it, 1], f_send.at[4 * it + 1])
            drain(bstate.at[it, 1], f_send.at[4 * it + 3])

    drain(pk.at[0], h_send.at[0])
    drain(pk.at[1], h_send.at[1])
    for g in range(groups):
        part = pl.ds(2 * LB * g, 2 * LB)

        @pl.when(up)
        def _():
            drain(b_up.at[part], h_send.at[6 + 2 * g])

        @pl.when(down)
        def _():
            drain(b_down.at[part], h_send.at[7 + 2 * g])

    for it in range(ITERS):

        @pl.when(before)
        def _():
            drain(fstate.at[it, 1], w_send.at[2 * it])

        @pl.when(after)
        def _():
            drain(ends_own.at[it], w_send.at[2 * it + 1])


def local_part(nm, nl, nw, *args):
    (
        ensemble,
        weights,
        diffusivity,
        coupling,
        tl_steps,
        obs_cell,
        obs_window,
        obs_value,
        obs_weight,
        error_weight,
    ) = args
    members = 2 * nm
    lon = nm * LANES
    planes = nw // 2
    groups = members // LB
    anywhere = pl.BlockSpec(memory_space=pltpu.HBM)
    obs = [x.reshape(-1, LANES) for x in (obs_cell, obs_window, obs_value, obs_weight)]
    tile = (LB, LANES)
    state = (NV, *tile)

    def buf(*shape):
        return pltpu.VMEM(shape, F32)

    dma = pltpu.SemaphoreType.DMA
    return pl.pallas_call(
        functools.partial(kernel, nm, nl, nw),
        name="assimilate",
        out_shape=(
            pltpu.VMEM((1, 2, LB, lon), F32),
            pltpu.VMEM((1, *state), F32),
        ),
        in_specs=[anywhere] * 4 + [pl.BlockSpec(memory_space=pltpu.SMEM)] + [anywhere] * 5,
        out_specs=(pl.BlockSpec(memory_space=pltpu.VMEM),)*2,
        scratch_shapes=[
            pltpu.SMEM((NV, NV), F32),
            pltpu.SMEM((NV,), F32),
            pltpu.VMEM(obs[0].shape, jnp.int32),
            pltpu.VMEM(obs[0].shape, jnp.int32),
            buf(*obs[0].shape),
            buf(*obs[0].shape),
            buf(NV, members, *tile),
            buf(2, LB, lon),
            buf(2, LB, lon),
            buf(4, lon),
            buf(4, lon),
            buf(members, *tile),
            buf(4, lon),
            buf(4, lon),
            buf(3, *state),
            buf(ITERS, 3, *state),
            buf(ITERS, 3, *state),
            buf(ITERS, *state),
            buf(ITERS, 3, *state),
            buf(ITERS, 3, *state),
            buf(2 * NV * LB, LANES),
            buf(*state),
            buf(2 * members, LANES),
            buf(2 * members, LANES),
            buf(NV, 2, 2 * members, LANES),
            buf(members * LB, LANES),
            buf(2, 2 * members, LANES),
            buf(2 * members, LANES),
            buf(2 * members, LANES),
            buf(2, 2 * members, LANES),
            buf(2, 2, *tile),
            buf(2, 2, *tile),
            buf(2, 2, *tile),
            buf(members * LB, LANES),
            buf(nm, 3, *tile),
            buf(3, LB, lon),
            dma((12,)),
            dma,
            dma,
            dma((planes,)),
            dma((planes,)),
            dma((planes,)),
            dma((planes,)),
            dma((3,)),
            dma((3,)),
            dma((2,)),
            dma((2,)),
            dma((4 * ITERS,)),
            dma((4 * ITERS,)),
            dma((2 * ITERS,)),
            dma((2 * ITERS,)),
            dma((2,)),
            dma((2,)),
            dma((planes,)),
            dma((planes,)),
            dma((planes,)),
            dma((planes,)),
            dma((2 * groups + 6,)),
            dma((2 * groups + 6,)),
            dma,
            dma,
        ],
        compiler_params=pltpu.CompilerParams(
            collective_id=0, has_side_effects=True, vmem_limit_bytes=40 * 1024 * 1024
        ),
    )(
        *(pltpu.with_memory_space_constraint(x, pltpu.HBM) for x in (ensemble, weights, diffusivity, coupling)),
        tl_steps,
        *(pltpu.with_memory_space_constraint(x, pltpu.HBM) for x in (*obs, error_weight)),
    )


def solution(mesh):
    sizes = [mesh.shape[axis] for axis in ("mem", "lat", "win")]
    return jax.shard_map(
        functools.partial(local_part, *sizes),
        mesh=mesh,
        in_specs=(
            P("mem", None, "lat", None),
            P("win", "mem", "lat", None),
            P(None, "lat", "mem"),
            P(),
            P("win"),
            P(("mem", "lat")),
            P(("mem", "lat")),
            P(("mem", "lat")),
            P(("mem", "lat")),
            P(),
        ),
        out_specs=(P("win", "mem", "lat", None), P("win", None, "lat", "mem")),
        check_vma=False,
    )
```
